128 devices in a mesh: tm: 16 (over x, y), space: 8 (over z, core).
Axes of the slice: x: 4, y: 4, z: 4, core: 2. Of those that a mesh axis runs over, the one named last changes fastest.
Arguments:
- video: bfloat16 [64, 1152, 1536], P('tm', 'space'), may hold values from -6 to 6
- frame_count: int32 [1], replicated, may hold values from 16 to 64
- qkv_space: bfloat16 [1536, 3072], replicated, may hold values from -0.15625 to 0.15625
- out_space: bfloat16 [1024, 1536], replicated, may hold values from -0.1875 to 0.1875
- qkv_time: bfloat16 [1536, 3072], replicated, may hold values from -0.15625 to 0.15625
- out_time: bfloat16 [1024, 1536], replicated, may hold values from -0.1875 to 0.1875
Outputs:
- encoded: bfloat16 [64, 1152, 1536], P('tm', 'space')
The draws below stay inside these ranges and needn't reach their ends.
All inputs are finite; a program needn't handle non-finite values.
Results may differ from the reference program's by a relative error of at most 0.0085.
Values may be sent and summed in bfloat16 or wider, within the bound.
No kernel may reach another device: no remote copies, remote signals or barrier semaphores. Data moves between devices by JAX's collectives and lax.ppermute only.
A program may use at most 192 MiB of HBM per device.

```python
import jax
import jax.numpy as jnp
from jax import lax

D = 1536
H = 16
HD = 64
PATCHES = 1152
FRAMES = 64


def block_scale(own_key, extent, pieces, low, top_value):
    level = 1.0
    for position, shards_of in pieces:
        steps = jax.random.uniform(jax.random.fold_in(jax.random.fold_in(own_key, 6), position), (shards_of,), jnp.float32, low / len(pieces), top_value / len(pieces))
        level = level * jnp.repeat(jnp.exp(steps), extent[position] // shards_of).reshape((-1,) + (1,) * (len(extent) - 1 - position))
    return level


def centred(key, shape, deviation, reach, cuts=(), held_as=jnp.bfloat16):
    drawn = jax.random.normal(key, shape, jnp.float32) * deviation
    if len(cuts) > 0:
        drawn = block_scale(key, shape, cuts, -0.22, 0.18) * drawn
    return jnp.clip(drawn, min=-reach, max=reach).astype(held_as)


def setup_inputs(seed: int = 0) -> dict:
    splits = jax.random.split(jax.random.key(seed), 7)
    video = centred(splits[0], (FRAMES, PATCHES, D), 1.0, 6.0, ((0, 16), (1, 8)))
    frame_count = jax.random.randint(splits[1], (1,), FRAMES // 4, FRAMES + 1).astype(jnp.int32)
    qkv_space = centred(splits[2], (D, 3 * H * HD), D ** -0.5, 0.15625)
    out_space = centred(splits[3], (H * HD, D), (H * HD) ** -0.5, 0.1875)
    qkv_time = centred(splits[4], (D, 3 * H * HD), D ** -0.5, 0.15625)
    out_time = centred(splits[5], (H * HD, D), (H * HD) ** -0.5, 0.1875)
    return dict(video=video, frame_count=frame_count, qkv_space=qkv_space, out_space=out_space, qkv_time=qkv_time, out_time=out_time)


def layer_norm(values):
    wide = values.astype(jnp.float32)
    center = wide - lax.optimization_barrier(jnp.mean(wide, axis=-1, keepdims=True))
    spread = lax.optimization_barrier(jnp.mean(center * center, axis=-1, keepdims=True))
    return (center * lax.rsqrt(spread + 1e-06)).astype(jnp.bfloat16)

def reference(video, frame_count, qkv_space, out_space, qkv_time, out_time):
    frames, patches, width = video.shape
    valid_keys = jnp.arange(frames) < frame_count[0]
    valid = valid_keys.astype(jnp.float32)[:, None, None]
    norm1 = layer_norm(video)
    qkv1 = jnp.dot(norm1.reshape(frames * patches, width), qkv_space, preferred_element_type=jnp.float32)
    qkv1 = qkv1.astype(jnp.bfloat16).reshape(frames, patches, 3, H, HD)

    def frame_attend(item):
        query = item[:, 0].astype(jnp.float32)
        keys = item[:, 1].astype(jnp.float32)
        values = item[:, 2].astype(jnp.float32)
        scores = jnp.einsum('qhd,khd->hqk', query, keys) * 0.125
        weights = jax.nn.softmax(scores, axis=-1).astype(jnp.bfloat16)
        result = jnp.einsum('hqk,khd->qhd', weights.astype(jnp.float32), values)
        return result.astype(jnp.bfloat16).reshape(patches, H * HD)
    spatial = lax.map(frame_attend, qkv1)
    branch = jnp.dot(spatial.reshape(frames * patches, H * HD), out_space, preferred_element_type=jnp.float32)
    middle = (video.astype(jnp.float32) + valid * branch.reshape(frames, patches, width)).astype(jnp.bfloat16)
    norm2 = layer_norm(middle)
    qkv2 = jnp.dot(norm2.reshape(frames * patches, width), qkv_time, preferred_element_type=jnp.float32)
    qkv2 = qkv2.astype(jnp.bfloat16).reshape(frames, patches, 3, H, HD)
    query = qkv2[:, :, 0].astype(jnp.float32)
    keys = qkv2[:, :, 1].astype(jnp.float32)
    values = qkv2[:, :, 2].astype(jnp.float32)
    scores = jnp.einsum('fphd,gphd->phfg', query, keys) * 0.125
    scores = jnp.where(valid_keys[None, None, None, :], scores, -1e+30)
    weights = jax.nn.softmax(scores, axis=-1).astype(jnp.bfloat16)
    temporal = jnp.einsum('phfg,gphd->fphd', weights.astype(jnp.float32), values)
    temporal = temporal.astype(jnp.bfloat16).reshape(frames * patches, H * HD)
    branch2 = jnp.dot(temporal, out_time, preferred_element_type=jnp.float32).reshape(frames, patches, width)
    return (middle.astype(jnp.float32) + valid * branch2).astype(jnp.bfloat16)
```

```python
import functools

import jax
import jax.numpy as jnp
from jax import lax
from jax.experimental import pallas as pl
from jax.experimental.pallas import tpu as pltpu
from jax.sharding import PartitionSpec as P

H = 16
HD = 64
WIDTH = 1536
HW = H * HD
TM = 16
QSCALE = 0.125 * 1.4426950408889634
CHUNKS = (9,)
OFFSETS = tuple(sum(CHUNKS[:j]) for j in range(len(CHUNKS)))
SWAP = [(i, i ^ 1) for i in range(8)]
Z_GROUPS = [[0, 2, 4, 6], [1, 3, 5, 7]]
BF = jnp.bfloat16
F32 = jnp.float32
VMEM = 56 * 1024 * 1024


def params(**more):
    return pltpu.CompilerParams(vmem_limit_bytes=VMEM, **more)


def normalise(wide):
    center = wide - jnp.mean(wide, axis=-1, keepdims=True)
    spread = jnp.mean(center * center, axis=-1, keepdims=True)
    return (center * lax.rsqrt(spread + 1e-06)).astype(BF)


def nt_dot(a, b):
    return lax.dot_general(a, b, (((1,), (1,)), ((), ())), preferred_element_type=F32)


def tn_dot(a, b):
    return lax.dot_general(a, b, (((0,), (0,)), ((), ())), preferred_element_type=F32)


def kv_kernel(x_ref, w_ref, kv_ref, norm_ref):
    @pl.when(pl.program_id(0) == 0)
    def _():
        def step(i, carry):
            rows = pl.ds(pl.multiple_of(i * 64, 64), 64)
            norm_ref[rows, :] = normalise(x_ref[rows, :].astype(F32))
            return carry

        lax.fori_loop(0, x_ref.shape[0] // 64, step, 0)

    kv_ref[...] = jnp.dot(norm_ref[...], w_ref[...], preferred_element_type=F32).astype(BF)


def keys_values(x, w):
    rows = x.shape[0]
    return pl.pallas_call(
        kv_kernel,
        grid=(4,),
        in_specs=[
            pl.BlockSpec((rows, WIDTH), lambda j: (0, 0)),
            pl.BlockSpec((WIDTH, 512), lambda j: (0, j + 2)),
        ],
        out_specs=[
            pl.BlockSpec((rows, 512), lambda j: (0, j)),
            pl.BlockSpec((rows, WIDTH), lambda j: (0, 0)),
        ],
        out_shape=[
            jax.ShapeDtypeStruct((rows, 2 * HW), BF),
            jax.ShapeDtypeStruct((rows, WIDTH), BF),
        ],
        compiler_params=params(),
        cost_estimate=pl.CostEstimate(
            flops=2 * rows * WIDTH * 2 * HW, bytes_accessed=12_000_000, transcendentals=0
        ),
        name="keys_values",
    )(x, w)


def q_kernel(norm_ref, w_ref, *q_refs):
    q = jnp.dot(norm_ref[...], w_ref[...], preferred_element_type=F32) * QSCALE
    q = q.astype(BF)
    for n, off, q_ref in zip(CHUNKS, OFFSETS, q_refs):
        for z in range(4):
            lo = z * 144 + off * 16
            q_ref[z] = q[lo : lo + n * 16]


def queries(norm, w):
    rows = norm.shape[0]
    return pl.pallas_call(
        q_kernel,
        grid=(2,),
        in_specs=[
            pl.BlockSpec((rows, WIDTH), lambda j: (0, 0)),
            pl.BlockSpec((WIDTH, 512), lambda j: (0, j)),
        ],
        out_specs=[pl.BlockSpec((4, 16 * n, 512), lambda j: (0, 0, j)) for n in CHUNKS],
        out_shape=[jax.ShapeDtypeStruct((4, 16 * n, HW), BF) for n in CHUNKS],
        compiler_params=params(),
        cost_estimate=pl.CostEstimate(
            flops=2 * rows * WIDTH * HW, bytes_accessed=6_000_000, transcendentals=0
        ),
        name="queries",
    )(norm, w)


def spatial_kernel(block, q_ref, ka_ref, kb_ref, va_ref, vb_ref, o_ref, kk, v0, v1):
    half = ka_ref.shape[0]
    low_v = lax.broadcasted_iota(jnp.int32, (half, 128), 1) < HD
    one = jnp.ones((half, 128), BF)
    for part, (k_ref, v_ref) in enumerate(((ka_ref, va_ref), (kb_ref, vb_ref))):
        rows = slice(part * half, (part + 1) * half)
        kk[rows, :] = k_ref[...]
        v = v_ref[...]
        v0[rows, :] = jnp.where(low_v, v, one)
        v1[rows, :] = jnp.where(low_v, one, v)
    low = lax.broadcasted_iota(jnp.int32, (block, 128), 1) < HD
    zero = jnp.zeros((block, 128), BF)

    def attend(q, v):
        s = nt_dot(q, kk[...])
        p = jnp.exp2(s - jnp.max(s, axis=-1, keepdims=True)).astype(BF)
        return jnp.dot(p, v[...], preferred_element_type=F32)

    def step(i, carry):
        rows = pl.ds(pl.multiple_of(i * block, block), block)
        q = q_ref[rows, :]
        o0 = attend(jnp.where(low, q, zero), v0)
        o1 = attend(jnp.where(low, zero, q), v1)
        top = jnp.where(low, o0, o1)
        total = pltpu.roll(jnp.where(low, o1, o0), HD, 1)
        o_ref[rows, :] = (top / total).astype(BF)
        return carry

    lax.fori_loop(0, q_ref.shape[0] // block, step, 0)


def spatial_attention(q, kv_a, kv_b, block):
    rows, half = q.shape[0], kv_a.shape[0]
    pairs = H // 2
    return pl.pallas_call(
        functools.partial(spatial_kernel, block),
        grid=(pairs,),
        in_specs=[
            pl.BlockSpec((rows, 128), lambda h: (0, h)),
            pl.BlockSpec((half, 128), lambda h: (0, h)),
            pl.BlockSpec((half, 128), lambda h: (0, h)),
            pl.BlockSpec((half, 128), lambda h: (0, h + pairs)),
            pl.BlockSpec((half, 128), lambda h: (0, h + pairs)),
        ],
        out_specs=pl.BlockSpec((rows, 128), lambda h: (0, h)),
        out_shape=jax.ShapeDtypeStruct((rows, HW), BF),
        scratch_shapes=[pltpu.VMEM((2 * half, 128), BF)] * 3,
        compiler_params=params(),
        cost_estimate=pl.CostEstimate(
            flops=16 * rows * half * HW, bytes_accessed=8_000_000, transcendentals=2 * rows * half * H
        ),
        name="spatial_attention",
    )(q, kv_a, kv_b, kv_a, kv_b)


def reorder(to_patch_major):
    row = lax.broadcasted_iota(jnp.int32, (64, 64), 0)
    col = lax.broadcasted_iota(jnp.int32, (64, 64), 1)
    if to_patch_major:
        return (col == (row % 4) * 16 + row // 4).astype(BF)
    return (col == (row % 16) * 4 + row // 16).astype(BF)


def middle_kernel(off, n, scalars, s_ref, x_ref, w_ref, middle_ref, send_ref, norm):
    span = 16 * n
    first, limit = scalars[0], scalars[1]
    for f in range(4):
        valid = (first + f < limit).astype(F32)
        branch = jnp.dot(s_ref[f], w_ref[...], preferred_element_type=F32)
        x = x_ref[f, off * 16 : off * 16 + span, :].astype(F32)
        middle = (x + valid * branch).astype(BF)
        middle_ref[f] = middle
        norm[f] = normalise(middle.astype(F32))
    move = reorder(True)
    for b in range(n):
        rows = slice(b * 16, b * 16 + 16)
        block = jnp.concatenate([norm[f, rows, :] for f in range(4)], axis=0)
        moved = jnp.dot(move, block, preferred_element_type=F32).astype(BF)
        send_ref[rows] = moved.reshape(16, 4, WIDTH)


def middle_rows(scalars, spatial, video, w, off, n):
    span = 16 * n
    return pl.pallas_call(
        functools.partial(middle_kernel, off, n),
        in_specs=[
            pl.BlockSpec(memory_space=pltpu.SMEM),
            pl.BlockSpec(memory_space=pltpu.VMEM),
            pl.BlockSpec(memory_space=pltpu.VMEM),
            pl.BlockSpec(memory_space=pltpu.VMEM),
        ],
        out_specs=[
            pl.BlockSpec(memory_space=pltpu.VMEM),
            pl.BlockSpec(memory_space=pltpu.VMEM),
        ],
        out_shape=[
            jax.ShapeDtypeStruct((4, span, WIDTH), BF),
            jax.ShapeDtypeStruct((span, 4, WIDTH), BF),
        ],
        scratch_shapes=[pltpu.VMEM((4, span, WIDTH), BF)],
        compiler_params=params(),
        cost_estimate=pl.CostEstimate(
            flops=8 * span * HW * WIDTH, bytes_accessed=8_000_000, transcendentals=0
        ),
        name="middle_rows",
    )(scalars, spatial, video, w)


def temporal_kernel(n, scalars, x_ref, wq_ref, wk_ref, wv_ref, o_ref, rows_ref):
    @pl.when(pl.program_id(0) == 0)
    def _():
        for i in range(n):
            rows_ref[64 * i : 64 * i + 64, :] = x_ref[:, i].reshape(64, WIDTH)

    limit = scalars[1]
    x = rows_ref[...]
    q = (jnp.dot(x, wq_ref[...], preferred_element_type=F32) * QSCALE).astype(BF)
    k = jnp.dot(x, wk_ref[...], preferred_element_type=F32).astype(BF)
    v = jnp.dot(x, wv_ref[...], preferred_element_type=F32).astype(BF)
    head_row = lax.broadcasted_iota(jnp.int32, (256, 256), 0) // HD
    head_col = lax.broadcasted_iota(jnp.int32, (256, 256), 1) // HD
    same = head_row == head_col
    zero = jnp.zeros((256, 256), BF)
    key_valid = lax.broadcasted_iota(jnp.int32, (4, 64, 64), 1) < limit
    for i in range(n):
        rows = slice(64 * i, 64 * i + 64)
        k4 = jnp.where(same, jnp.concatenate([k[rows]] * 4, axis=0), zero)
        v4 = jnp.where(same, jnp.concatenate([v[rows]] * 4, axis=0), zero)
        s = nt_dot(k4, q[rows]).reshape(4, 64, 64)
        s = jnp.where(key_valid, s, -1e30)
        p = jnp.exp2(s - jnp.max(s, axis=1, keepdims=True))
        p = (p / jnp.sum(p, axis=1, keepdims=True)).reshape(256, 64).astype(BF)
        o_ref[:, i] = tn_dot(p, v4).astype(BF).reshape(16, 4, 256)


def temporal_attention(scalars, x, w, n):
    rows = 64 * n
    return pl.pallas_call(
        functools.partial(temporal_kernel, n),
        grid=(4,),
        in_specs=[
            pl.BlockSpec(memory_space=pltpu.SMEM),
            pl.BlockSpec((TM, n, 4, WIDTH), lambda g: (0, 0, 0, 0)),
            pl.BlockSpec((WIDTH, 256), lambda g: (0, g)),
            pl.BlockSpec((WIDTH, 256), lambda g: (0, g + 4)),
            pl.BlockSpec((WIDTH, 256), lambda g: (0, g + 8)),
        ],
        out_specs=pl.BlockSpec((TM, n, 4, 256), lambda g: (0, 0, 0, g)),
        out_shape=jax.ShapeDtypeStruct((TM, n, 4, HW), BF),
        scratch_shapes=[pltpu.VMEM((rows, WIDTH), BF)],
        compiler_params=params(),
        cost_estimate=pl.CostEstimate(
            flops=2 * rows * WIDTH * 3 * HW, bytes_accessed=14_000_000, transcendentals=0
        ),
        name="temporal_attention",
    )(scalars, x, w, w, w)


def encoded_kernel(scalars, *refs):
    count = len(CHUNKS)
    t_refs, m_refs = refs[:count], refs[count : 2 * count]
    w_ref, o_ref, rows_ref = refs[2 * count :]

    @pl.when(pl.program_id(0) == 0)
    def _():
        move = reorder(False)
        for n, off, t_ref in zip(CHUNKS, OFFSETS, t_refs):
            for b in range(n):
                block = t_ref[b * 16 : b * 16 + 16].reshape(64, HW)
                moved = jnp.dot(move, block, preferred_element_type=F32).astype(BF)
                for f in range(4):
                    lo = (off + b) * 16
                    rows_ref[f, lo : lo + 16, :] = moved[f * 16 : f * 16 + 16]

    first, limit = scalars[0], scalars[1]
    for f in range(4):
        valid = (first + f < limit).astype(F32)
        branch = jnp.dot(rows_ref[f], w_ref[...], preferred_element_type=F32)
        for n, off, m_ref in zip(CHUNKS, OFFSETS, m_refs):
            rows = slice(off * 16, (off + n) * 16)
            o_ref[f, rows, :] = (m_ref[f].astype(F32) + valid * branch[rows]).astype(BF)


def encoded_rows(scalars, temporals, middles, w):
    columns = 512
    return pl.pallas_call(
        encoded_kernel,
        grid=(WIDTH // columns,),
        in_specs=[pl.BlockSpec(memory_space=pltpu.SMEM)]
        + [pl.BlockSpec((16 * n, 4, HW), lambda j: (0, 0, 0)) for n in CHUNKS]
        + [pl.BlockSpec((4, 16 * n, columns), lambda j: (0, 0, j)) for n in CHUNKS]
        + [pl.BlockSpec((HW, columns), lambda j: (0, j))],
        out_specs=pl.BlockSpec((4, 144, columns), lambda j: (0, 0, j)),
        out_shape=jax.ShapeDtypeStruct((4, 144, WIDTH), BF),
        scratch_shapes=[pltpu.VMEM((4, 144, HW), BF)],
        compiler_params=params(),
        cost_estimate=pl.CostEstimate(
            flops=8 * 144 * HW * WIDTH, bytes_accessed=8_000_000, transcendentals=0
        ),
        name="encoded_rows",
    )(scalars, *temporals, *middles, w)


def over_z(x):
    return lax.all_to_all(
        x, "space", split_axis=0, concat_axis=0, axis_index_groups=Z_GROUPS, tiled=True
    )


def over_tm(x):
    return lax.all_to_all(x, "tm", split_axis=0, concat_axis=0, tiled=True)


def per_device(video, frame_count, qkv_space, out_space, qkv_time, out_time):
    first = lax.axis_index("tm") * video.shape[0]
    scalars = jnp.stack([first, frame_count[0]]).astype(jnp.int32)
    frame = over_z(video).reshape(4 * 144, WIDTH)
    kv_own, norm1 = keys_values(frame, qkv_space)
    kv_other = lax.ppermute(kv_own, "space", SWAP)
    qs = queries(norm1, qkv_space)
    temporals, middles = [], []
    for n, off, q in zip(CHUNKS, OFFSETS, qs):
        spatial = spatial_attention(q.reshape(64 * n, HW), kv_own, kv_other, 192 if n % 3 == 0 else 64 * n)
        spatial = over_z(spatial.reshape(4, 16 * n, HW))
        middle, send = middle_rows(scalars, spatial, video, out_space, off, n)
        middles.append(middle)
        rows = over_tm(send.reshape(TM, n, 4, WIDTH))
        temporal = temporal_attention(scalars, rows, qkv_time, n)
        temporals.append(over_tm(temporal).reshape(16 * n, 4, HW))
    return encoded_rows(scalars, temporals, middles, out_time)


def solution(mesh):
    return jax.shard_map(
        per_device,
        mesh=mesh,
        in_specs=(P("tm", "space", None), P(), P(), P(), P(), P()),
        out_specs=P("tm", "space", None),
        check_vma=False,
    )
```

```python
import functools

import jax
import jax.numpy as jnp
from jax import lax
from jax.experimental import pallas as pl
from jax.experimental.pallas import tpu as pltpu
from jax.sharding import PartitionSpec as P

H = 16
HD = 64
WIDTH = 1536
HW = H * HD
TM = 16
QSCALE = 0.125 * 1.4426950408889634
CHUNKS = (9,)
SUB = {9: 144, 5: 160, 4: 128, 3: 96}
OFFSETS = tuple(sum(CHUNKS[:j]) for j in range(len(CHUNKS)))
SWAP = [(i, i ^ 1) for i in range(8)]
Z_GROUPS = [[0, 2, 4, 6], [1, 3, 5, 7]]
BF = jnp.bfloat16
F32 = jnp.float32


def params(mebibytes):
    return pltpu.CompilerParams(vmem_limit_bytes=mebibytes * 1024 * 1024)


def normalise(wide):
    center = wide - jnp.mean(wide, axis=-1, keepdims=True)
    spread = jnp.mean(center * center, axis=-1, keepdims=True)
    return (center * lax.rsqrt(spread + 1e-06)).astype(BF)


def nt_dot(a, b):
    return lax.dot_general(a, b, (((1,), (1,)), ((), ())), preferred_element_type=F32)


def tn_dot(a, b):
    return lax.dot_general(a, b, (((0,), (0,)), ((), ())), preferred_element_type=F32)


def kv_kernel(scalars, x_ref, w_ref, kv_ref, norm_ref):
    @pl.when(pl.program_id(0) == 0)
    def _():
        def step(i, carry):
            rows = pl.ds(pl.multiple_of(i * 64, 64), 64)
            norm_ref[rows, :] = normalise(x_ref[rows, :].astype(F32))
            return carry

        lax.fori_loop(0, x_ref.shape[0] // 64, step, 0)

    kv_ref[...] = jnp.dot(norm_ref[...], w_ref[...], preferred_element_type=F32).astype(BF)


def keys_values(scalars, x, w):
    rows = x.shape[0]
    return pl.pallas_call(
        kv_kernel,
        grid=(4,),
        in_specs=[
            pl.BlockSpec(memory_space=pltpu.SMEM),
            pl.BlockSpec((rows, WIDTH), lambda j: (0, 0)),
            pl.BlockSpec((WIDTH, 512), lambda j: (0, j + 2)),
        ],
        out_specs=[
            pl.BlockSpec((rows, 512), lambda j: (0, j)),
            pl.BlockSpec((rows, WIDTH), lambda j: (0, 0)),
        ],
        out_shape=[
            jax.ShapeDtypeStruct((rows, 2 * HW), BF),
            jax.ShapeDtypeStruct((rows, WIDTH), BF),
        ],
        compiler_params=params(24),
        cost_estimate=pl.CostEstimate(
            flops=2 * rows * WIDTH * 2 * HW, bytes_accessed=12_000_000, transcendentals=0
        ),
        name="keys_values",
    )(scalars, x, w)


def q_kernel(norm_ref, w_ref, *q_refs):
    q = jnp.dot(norm_ref[...], w_ref[...], preferred_element_type=F32) * QSCALE
    q = q.astype(BF)
    for n, off, q_ref in zip(CHUNKS, OFFSETS, q_refs):
        for z in range(4):
            lo = z * 144 + off * 16
            q_ref[z] = q[lo : lo + n * 16]


def queries(norm, w):
    rows = norm.shape[0]
    return pl.pallas_call(
        q_kernel,
        grid=(2,),
        in_specs=[
            pl.BlockSpec((rows, WIDTH), lambda j: (0, 0)),
            pl.BlockSpec((WIDTH, 512), lambda j: (0, j)),
        ],
        out_specs=[pl.BlockSpec((4, 16 * n, 512), lambda j: (0, 0, j)) for n in CHUNKS],
        out_shape=[jax.ShapeDtypeStruct((4, 16 * n, HW), BF) for n in CHUNKS],
        compiler_params=params(24),
        cost_estimate=pl.CostEstimate(
            flops=2 * rows * WIDTH * HW, bytes_accessed=6_000_000, transcendentals=0
        ),
        name="queries",
    )(norm, w)


def spatial_kernel(sub, q_ref, ka_ref, kb_ref, va_ref, vb_ref, o_ref, keys, values, s_a, s_b, m_a, m_b):
    rows, half = q_ref.shape[0], ka_ref.shape[0]
    count, pairs = rows // sub, H // 2
    low = lax.broadcasted_iota(jnp.int32, (sub, 128), 1) < HD
    zero = jnp.zeros((sub, 128), BF)
    values[:, 128:] = jnp.ones((2 * half, 128), BF)

    def columns(pair):
        return pl.ds(pl.multiple_of(pair * 128, 128), 128)

    def load(pair, a_ref, b_ref, held):
        held[:half, :128] = a_ref[:, columns(pair)]
        held[half:, :128] = b_ref[:, columns(pair)]

    def score(pair, head, i, s_ref, m_ref):
        part = slice(i * sub, (i + 1) * sub)
        q = q_ref[part, columns(pair)]
        q = jnp.where(low, q, zero) if head == 0 else jnp.where(low, zero, q)
        s = nt_dot(q, keys[...])
        s_ref[part, :] = s
        m_ref[part, :] = jnp.broadcast_to(jnp.max(s, axis=-1, keepdims=True), (sub, 128))

    def weigh(i, s_ref, m_ref):
        part = slice(i * sub, (i + 1) * sub)
        p = jnp.exp2(s_ref[part, :] - m_ref[part, :1]).astype(BF)
        o = jnp.dot(p, values[...], preferred_element_type=F32)
        return o[:, :128] / o[:, 128:]

    load(0, ka_ref, kb_ref, keys)
    for i in range(count):
        score(0, 0, i, s_a, m_a)

    def step(pair, carry):
        load(pair, va_ref, vb_ref, values)
        first = []
        for i in range(count):
            score(pair, 1, i, s_b, m_b)
            first.append(weigh(i, s_a, m_a))
        later = jnp.minimum(pair + 1, pairs - 1)
        load(later, ka_ref, kb_ref, keys)
        for i in range(count):
            score(later, 0, i, s_a, m_a)
            second = weigh(i, s_b, m_b)
            o_ref[i * sub : (i + 1) * sub, columns(pair)] = jnp.where(low, first[i], second).astype(BF)
        return carry

    lax.fori_loop(0, pairs, step, 0)


def spatial_attention(q, kv_a, kv_b, sub):
    rows, half = q.shape[0], kv_a.shape[0]
    k_spec = pl.BlockSpec((half, HW), lambda i: (0, 0))
    v_spec = pl.BlockSpec((half, HW), lambda i: (0, 1))
    return pl.pallas_call(
        functools.partial(spatial_kernel, sub),
        grid=(1,),
        in_specs=[pl.BlockSpec((rows, HW), lambda i: (0, 0)), k_spec, k_spec, v_spec, v_spec],
        out_specs=pl.BlockSpec((rows, HW), lambda i: (0, 0)),
        out_shape=jax.ShapeDtypeStruct((rows, HW), BF),
        scratch_shapes=[pltpu.VMEM((2 * half, 128), BF), pltpu.VMEM((2 * half, 256), BF)]
        + [pltpu.VMEM((rows, 2 * half), F32)] * 2
        + [pltpu.VMEM((rows, 128), F32)] * 2,
        compiler_params=params(32),
        cost_estimate=pl.CostEstimate(
            flops=40 * rows * half * HW, bytes_accessed=8_000_000, transcendentals=2 * rows * half * H
        ),
        name="spatial_attention",
    )(q, kv_a, kv_b, kv_a, kv_b)


def reorder(to_patch_major):
    row = lax.broadcasted_iota(jnp.int32, (64, 64), 0)
    col = lax.broadcasted_iota(jnp.int32, (64, 64), 1)
    if to_patch_major:
        return (col == (row % 4) * 16 + row // 4).astype(BF)
    return (col == (row % 16) * 4 + row // 16).astype(BF)


def middle_kernel(off, n, scalars, s_ref, x_ref, w_ref, middle_ref, send_ref, norm):
    span = 16 * n
    first, limit = scalars[0], scalars[1]
    for f in range(4):
        valid = (first + f < limit).astype(F32)
        branch = jnp.dot(s_ref[f], w_ref[...], preferred_element_type=F32)
        x = x_ref[f, off * 16 : off * 16 + span, :].astype(F32)
        middle = (x + valid * branch).astype(BF)
        middle_ref[f] = middle
        norm[f] = normalise(middle.astype(F32))
    move = reorder(True)
    for b in range(n):
        rows = slice(b * 16, b * 16 + 16)
        block = jnp.concatenate([norm[f, rows, :] for f in range(4)], axis=0)
        moved = jnp.dot(move, block, preferred_element_type=F32).astype(BF)
        send_ref[rows] = moved.reshape(16, 4, WIDTH)


def middle_rows(scalars, spatial, video, w, off, n):
    span = 16 * n
    return pl.pallas_call(
        functools.partial(middle_kernel, off, n),
        in_specs=[
            pl.BlockSpec(memory_space=pltpu.SMEM),
            pl.BlockSpec(memory_space=pltpu.VMEM),
            pl.BlockSpec(memory_space=pltpu.VMEM),
            pl.BlockSpec(memory_space=pltpu.VMEM),
        ],
        out_specs=[
            pl.BlockSpec(memory_space=pltpu.VMEM),
            pl.BlockSpec(memory_space=pltpu.VMEM),
        ],
        out_shape=[
            jax.ShapeDtypeStruct((4, span, WIDTH), BF),
            jax.ShapeDtypeStruct((span, 4, WIDTH), BF),
        ],
        scratch_shapes=[pltpu.VMEM((4, span, WIDTH), BF)],
        compiler_params=params(24),
        cost_estimate=pl.CostEstimate(
            flops=8 * span * HW * WIDTH, bytes_accessed=8_000_000, transcendentals=0
        ),
        name="middle_rows",
    )(scalars, spatial, video, w)


def temporal_kernel(n, scalars, x_ref, wq_ref, wk_ref, wv_ref, o_ref, rows_ref):
    @pl.when(pl.program_id(0) == 0)
    def _():
        for i in range(n):
            rows_ref[64 * i : 64 * i + 64, :] = x_ref[:, i].reshape(64, WIDTH)

    limit = scalars[1]
    x = rows_ref[...]
    q = (jnp.dot(x, wq_ref[...], preferred_element_type=F32) * QSCALE).astype(BF)
    k = jnp.dot(x, wk_ref[...], preferred_element_type=F32).astype(BF)
    v = jnp.dot(x, wv_ref[...], preferred_element_type=F32).astype(BF)
    head_row = lax.broadcasted_iota(jnp.int32, (256, 256), 0) // HD
    head_col = lax.broadcasted_iota(jnp.int32, (256, 256), 1) // HD
    same = head_row == head_col
    zero = jnp.zeros((256, 256), BF)
    key_valid = lax.broadcasted_iota(jnp.int32, (4, 64, 64), 1) < limit
    scores, weights = [], []
    for i in range(n):
        rows = slice(64 * i, 64 * i + 64)
        k4 = jnp.where(same, jnp.concatenate([k[rows]] * 4, axis=0), zero)
        scores.append(nt_dot(k4, q[rows]).reshape(4, 64, 64))
    for i in range(n):
        s = jnp.where(key_valid, scores[i], -1e30)
        p = jnp.exp2(s - jnp.max(s, axis=1, keepdims=True))
        p = p / jnp.sum(p, axis=1, keepdims=True)
        weights.append(p.reshape(256, 64).astype(BF))
    for i in range(n):
        rows = slice(64 * i, 64 * i + 64)
        v4 = jnp.where(same, jnp.concatenate([v[rows]] * 4, axis=0), zero)
        o_ref[:, i] = tn_dot(weights[i], v4).astype(BF).reshape(16, 4, 256)


def temporal_attention(scalars, x, w, n):
    rows = 64 * n
    return pl.pallas_call(
        functools.partial(temporal_kernel, n),
        grid=(4,),
        in_specs=[
            pl.BlockSpec(memory_space=pltpu.SMEM),
            pl.BlockSpec((TM, n, 4, WIDTH), lambda g: (0, 0, 0, 0)),
            pl.BlockSpec((WIDTH, 256), lambda g: (0, g)),
            pl.BlockSpec((WIDTH, 256), lambda g: (0, g + 4)),
            pl.BlockSpec((WIDTH, 256), lambda g: (0, g + 8)),
        ],
        out_specs=pl.BlockSpec((TM, n, 4, 256), lambda g: (0, 0, 0, g)),
        out_shape=jax.ShapeDtypeStruct((TM, n, 4, HW), BF),
        scratch_shapes=[pltpu.VMEM((rows, WIDTH), BF)],
        compiler_params=params(24),
        cost_estimate=pl.CostEstimate(
            flops=2 * rows * WIDTH * 3 * HW, bytes_accessed=14_000_000, transcendentals=0
        ),
        name="temporal_attention",
    )(scalars, x, w, w, w)


def encoded_kernel(scalars, *refs):
    count = len(CHUNKS)
    t_refs, m_refs = refs[:count], refs[count : 2 * count]
    w_ref, o_ref, rows_ref = refs[2 * count :]

    @pl.when(pl.program_id(0) == 0)
    def _():
        move = reorder(False)
        for n, off, t_ref in zip(CHUNKS, OFFSETS, t_refs):
            for b in range(n):
                block = t_ref[b * 16 : b * 16 + 16].reshape(64, HW)
                moved = jnp.dot(move, block, preferred_element_type=F32).astype(BF)
                for f in range(4):
                    lo = (off + b) * 16
                    rows_ref[f, lo : lo + 16, :] = moved[f * 16 : f * 16 + 16]

    first, limit = scalars[0], scalars[1]
    for f in range(4):
        valid = (first + f < limit).astype(F32)
        branch = jnp.dot(rows_ref[f], w_ref[...], preferred_element_type=F32)
        for n, off, m_ref in zip(CHUNKS, OFFSETS, m_refs):
            rows = slice(off * 16, (off + n) * 16)
            o_ref[f, rows, :] = (m_ref[f].astype(F32) + valid * branch[rows]).astype(BF)


def encoded_rows(scalars, temporals, middles, w):
    columns = 512
    return pl.pallas_call(
        encoded_kernel,
        grid=(WIDTH // columns,),
        in_specs=[pl.BlockSpec(memory_space=pltpu.SMEM)]
        + [pl.BlockSpec((16 * n, 4, HW), lambda j: (0, 0, 0)) for n in CHUNKS]
        + [pl.BlockSpec((4, 16 * n, columns), lambda j: (0, 0, j)) for n in CHUNKS]
        + [pl.BlockSpec((HW, columns), lambda j: (0, j))],
        out_specs=pl.BlockSpec((4, 144, columns), lambda j: (0, 0, j)),
        out_shape=jax.ShapeDtypeStruct((4, 144, WIDTH), BF),
        scratch_shapes=[pltpu.VMEM((4, 144, HW), BF)],
        compiler_params=params(24),
        cost_estimate=pl.CostEstimate(
            flops=8 * 144 * HW * WIDTH, bytes_accessed=8_000_000, transcendentals=0
        ),
        name="encoded_rows",
    )(scalars, *temporals, *middles, w)


def over_z(x):
    return lax.all_to_all(
        x, "space", split_axis=0, concat_axis=0, axis_index_groups=Z_GROUPS, tiled=True
    )


def over_tm(x):
    return lax.all_to_all(x, "tm", split_axis=0, concat_axis=0, tiled=True)


def per_device(video, frame_count, qkv_space, out_space, qkv_time, out_time):
    first = lax.axis_index("tm") * video.shape[0]
    scalars = jnp.stack([first, frame_count[0]]).astype(jnp.int32)
    frame = over_z(video).reshape(4 * 144, WIDTH)
    kv_own, norm1 = keys_values(scalars, frame, qkv_space)
    kv_other = lax.ppermute(kv_own, "space", SWAP)
    qs = queries(norm1, qkv_space)
    temporals, middles = [], []
    for n, off, q in zip(CHUNKS, OFFSETS, qs):
        spatial = spatial_attention(q.reshape(64 * n, HW), kv_own, kv_other, SUB[n])
        spatial = over_z(spatial.reshape(4, 16 * n, HW))
        middle, send = middle_rows(scalars, spatial, video, out_space, off, n)
        middles.append(middle)
        rows = over_tm(send.reshape(TM, n, 4, WIDTH))
        temporal = temporal_attention(scalars, rows, qkv_time, n)
        temporals.append(over_tm(temporal).reshape(16 * n, 4, HW))
    return encoded_rows(scalars, temporals, middles, out_time)


def solution(mesh):
    return jax.shard_map(
        per_device,
        mesh=mesh,
        in_specs=(P("tm", "space", None), P(), P(), P(), P(), P()),
        out_specs=P("tm", "space", None),
        check_vma=False,
    )
```

```python
import functools

import jax
import jax.numpy as jnp
from jax import lax
from jax.experimental import pallas as pl
from jax.experimental.pallas import tpu as pltpu
from jax.sharding import PartitionSpec as P

H = 16
HD = 64
WIDTH = 1536
HW = H * HD
TM = 16
QSCALE = 0.125 * 1.4426950408889634
CHUNKS = (9,)
OFFSETS = tuple(sum(CHUNKS[:j]) for j in range(len(CHUNKS)))
SWAP = [(i, i ^ 1) for i in range(8)]
Z_GROUPS = [[0, 2, 4, 6], [1, 3, 5, 7]]
BF = jnp.bfloat16
F32 = jnp.float32


def params(mebibytes):
    return pltpu.CompilerParams(vmem_limit_bytes=mebibytes * 1024 * 1024)


def normalise(wide):
    center = wide - jnp.mean(wide, axis=-1, keepdims=True)
    spread = jnp.mean(center * center, axis=-1, keepdims=True)
    return (center * lax.rsqrt(spread + 1e-06)).astype(BF)


def nt_dot(a, b):
    return lax.dot_general(a, b, (((1,), (1,)), ((), ())), preferred_element_type=F32)


def tn_dot(a, b):
    return lax.dot_general(a, b, (((0,), (0,)), ((), ())), preferred_element_type=F32)


def kv_kernel(scalars, x_ref, w_ref, kv_ref, norm_ref):
    @pl.when(pl.program_id(0) == 0)
    def _():
        def step(i, carry):
            rows = pl.ds(pl.multiple_of(i * 64, 64), 64)
            norm_ref[rows, :] = normalise(x_ref[rows, :].astype(F32))
            return carry

        lax.fori_loop(0, x_ref.shape[0] // 64, step, 0)

    kv_ref[...] = jnp.dot(norm_ref[...], w_ref[...], preferred_element_type=F32).astype(BF)


def keys_values(scalars, x, w):
    rows = x.shape[0]
    return pl.pallas_call(
        kv_kernel,
        grid=(4,),
        in_specs=[
            pl.BlockSpec(memory_space=pltpu.SMEM),
            pl.BlockSpec((rows, WIDTH), lambda j: (0, 0)),
            pl.BlockSpec((WIDTH, 512), lambda j: (0, j + 2)),
        ],
        out_specs=[
            pl.BlockSpec((rows, 512), lambda j: (0, j)),
            pl.BlockSpec((rows, WIDTH), lambda j: (0, 0)),
        ],
        out_shape=[
            jax.ShapeDtypeStruct((rows, 2 * HW), BF),
            jax.ShapeDtypeStruct((rows, WIDTH), BF),
        ],
        compiler_params=params(24),
        cost_estimate=pl.CostEstimate(
            flops=2 * rows * WIDTH * 2 * HW, bytes_accessed=12_000_000, transcendentals=0
        ),
        name="keys_values",
    )(scalars, x, pltpu.with_memory_space_constraint(w, pltpu.HBM))


def q_kernel(norm_ref, w_ref, q_ref):
    q = jnp.dot(norm_ref[...], w_ref[...], preferred_element_type=F32) * QSCALE
    q_ref[...] = q.astype(BF)


def queries(norm, w):
    rows = norm.shape[0]
    return pl.pallas_call(
        q_kernel,
        grid=(2,),
        in_specs=[
            pl.BlockSpec((rows, WIDTH), lambda j: (0, 0)),
            pl.BlockSpec((WIDTH, 512), lambda j: (0, j)),
        ],
        out_specs=pl.BlockSpec((rows, 512), lambda j: (0, j)),
        out_shape=jax.ShapeDtypeStruct((rows, HW), BF),
        compiler_params=params(24),
        cost_estimate=pl.CostEstimate(
            flops=2 * rows * WIDTH * HW, bytes_accessed=6_000_000, transcendentals=0
        ),
        name="queries",
    )(norm, w)


def spatial_kernel(distance, scalars, q_ref, a_ref, b_ref, o_ref, keys, values, s_a, s_b, m_a, m_b):
    half, pairs = a_ref.shape[0], H // 2
    rows = o_ref.shape[0]
    own = lax.rem(scalars[2] + distance, 4)
    low = lax.broadcasted_iota(jnp.int32, (rows, 128), 1) < HD
    zero = jnp.zeros((rows, 128), BF)
    for e in range(2):
        values[e, :, 128:] = jnp.ones((2 * half, 128), BF)

    def columns(pair):
        return pl.ds(pl.multiple_of(pair * 128, 128), 128)

    def load(pair, held, e):
        held[e, :half, :128] = a_ref[:, columns(pair)]
        held[e, half:, :128] = b_ref[:, columns(pair)]

    def score(group, e, head, s_ref, m_ref):
        q = q_ref[own, :, columns(2 * group + e)]
        q = jnp.where(low, q, zero) if head == 0 else jnp.where(low, zero, q)
        s = nt_dot(q, keys[e])
        s_ref[2 * e + head] = s
        m_ref[2 * e + head] = jnp.broadcast_to(jnp.max(s, axis=-1, keepdims=True), (rows, 128))

    def weigh(e, head, s_ref, m_ref):
        p = jnp.exp2(s_ref[2 * e + head] - m_ref[2 * e + head, :, :1]).astype(BF)
        o = jnp.dot(p, values[e], preferred_element_type=F32)
        return o[:, :128] / o[:, 128:]

    def phase(group, later, s_now, m_now, s_next, m_next):
        for e in range(2):
            load(2 * group + e + pairs, values, e)
            load(2 * later + e, keys, e)
        for e in range(2):
            out = []
            for head in range(2):
                score(later, e, head, s_next, m_next)
                out.append(weigh(e, head, s_now, m_now))
            o_ref[:, columns(2 * group + e)] = jnp.where(low, out[0], out[1]).astype(BF)

    for e in range(2):
        load(e, keys, e)
        for head in range(2):
            score(0, e, head, s_a, m_a)

    def step(i, carry):
        phase(2 * i, 2 * i + 1, s_a, m_a, s_b, m_b)
        phase(2 * i + 1, jnp.minimum(2 * i + 2, pairs // 2 - 1), s_b, m_b, s_a, m_a)
        return carry

    lax.fori_loop(0, pairs // 4, step, 0)


def spatial_attention(scalars, q, kv_a, kv_b, distance):
    rows, total = q.shape[1], 2 * kv_a.shape[0]
    whole = pl.BlockSpec(memory_space=pltpu.VMEM)
    return pl.pallas_call(
        functools.partial(spatial_kernel, distance),
        in_specs=[pl.BlockSpec(memory_space=pltpu.SMEM), whole, whole, whole],
        out_specs=whole,
        out_shape=jax.ShapeDtypeStruct((rows, HW), BF),
        scratch_shapes=[pltpu.VMEM((2, total, 128), BF), pltpu.VMEM((2, total, 256), BF)]
        + [pltpu.VMEM((4, rows, total), F32)] * 2
        + [pltpu.VMEM((4, rows, 128), F32)] * 2,
        compiler_params=params(24),
        cost_estimate=pl.CostEstimate(
            flops=20 * rows * total * HW, bytes_accessed=6_000_000, transcendentals=rows * total * H
        ),
        name="spatial_attention",
    )(scalars, q, kv_a, kv_b)


def reorder(to_patch_major):
    row = lax.broadcasted_iota(jnp.int32, (64, 64), 0)
    col = lax.broadcasted_iota(jnp.int32, (64, 64), 1)
    if to_patch_major:
        return (col == (row % 4) * 16 + row // 4).astype(BF)
    return (col == (row % 16) * 4 + row // 16).astype(BF)


def middle_kernel(scalars, *refs):
    s_refs, (x_ref, w_ref, middle_ref, send_ref, norm) = refs[:4], refs[4:]
    first, limit, z = scalars[0], scalars[1], scalars[2]
    for d in range(4):
        f = lax.rem(z + 4 - d, 4)
        valid = (first + f < limit).astype(F32)
        branch = jnp.dot(s_refs[d][...], w_ref[...], preferred_element_type=F32)
        middle = (x_ref[f].astype(F32) + valid * branch).astype(BF)
        middle_ref[f] = middle
        norm[f] = normalise(middle.astype(F32))
    move = reorder(True)
    for b in range(9):
        rows = slice(b * 16, b * 16 + 16)
        block = jnp.concatenate([norm[f, rows, :] for f in range(4)], axis=0)
        moved = jnp.dot(move, block, preferred_element_type=F32).astype(BF)
        send_ref[rows] = moved.reshape(16, 4, WIDTH)


def middle_rows(scalars, blocks, video, w):
    whole = pl.BlockSpec(memory_space=pltpu.VMEM)
    return pl.pallas_call(
        middle_kernel,
        in_specs=[pl.BlockSpec(memory_space=pltpu.SMEM)] + [whole] * 6,
        out_specs=[whole, whole],
        out_shape=[
            jax.ShapeDtypeStruct((4, 144, WIDTH), BF),
            jax.ShapeDtypeStruct((144, 4, WIDTH), BF),
        ],
        scratch_shapes=[pltpu.VMEM((4, 144, WIDTH), BF)],
        compiler_params=params(24),
        cost_estimate=pl.CostEstimate(
            flops=8 * 144 * HW * WIDTH, bytes_accessed=8_000_000, transcendentals=0
        ),
        name="middle_rows",
    )(scalars, *blocks, video, w)


def temporal_kernel(n, scalars, x_ref, wq_ref, wk_ref, wv_ref, o_ref, rows_ref):
    @pl.when(pl.program_id(0) == 0)
    def _():
        for i in range(n):
            rows_ref[64 * i : 64 * i + 64, :] = x_ref[:, i].reshape(64, WIDTH)

    limit = scalars[1]
    x = rows_ref[...]
    q = (jnp.dot(x, wq_ref[...], preferred_element_type=F32) * QSCALE).astype(BF)
    k = jnp.dot(x, wk_ref[...], preferred_element_type=F32).astype(BF)
    v = jnp.dot(x, wv_ref[...], preferred_element_type=F32).astype(BF)
    head_row = lax.broadcasted_iota(jnp.int32, (256, 256), 0) // HD
    head_col = lax.broadcasted_iota(jnp.int32, (256, 256), 1) // HD
    same = head_row == head_col
    zero = jnp.zeros((256, 256), BF)
    key_valid = lax.broadcasted_iota(jnp.int32, (4, 64, 64), 1) < limit
    scores, weights = [], []
    for i in range(n):
        rows = slice(64 * i, 64 * i + 64)
        k4 = jnp.where(same, jnp.concatenate([k[rows]] * 4, axis=0), zero)
        scores.append(nt_dot(k4, q[rows]).reshape(4, 64, 64))
    for i in range(n):
        s = jnp.where(key_valid, scores[i], -1e30)
        p = jnp.exp2(s - jnp.max(s, axis=1, keepdims=True))
        p = p / jnp.sum(p, axis=1, keepdims=True)
        weights.append(p.reshape(256, 64).astype(BF))
    for i in range(n):
        rows = slice(64 * i, 64 * i + 64)
        v4 = jnp.where(same, jnp.concatenate([v[rows]] * 4, axis=0), zero)
        o_ref[:, i] = tn_dot(weights[i], v4).astype(BF).reshape(16, 4, 256)


def temporal_attention(scalars, x, w, n):
    rows = 64 * n
    return pl.pallas_call(
        functools.partial(temporal_kernel, n),
        grid=(4,),
        in_specs=[
            pl.BlockSpec(memory_space=pltpu.SMEM),
            pl.BlockSpec((TM, n, 4, WIDTH), lambda g: (0, 0, 0, 0)),
            pl.BlockSpec((WIDTH, 256), lambda g: (0, g)),
            pl.BlockSpec((WIDTH, 256), lambda g: (0, g + 4)),
            pl.BlockSpec((WIDTH, 256), lambda g: (0, g + 8)),
        ],
        out_specs=pl.BlockSpec((TM, n, 4, 256), lambda g: (0, 0, 0, g)),
        out_shape=jax.ShapeDtypeStruct((TM, n, 4, HW), BF),
        scratch_shapes=[pltpu.VMEM((rows, WIDTH), BF)],
        compiler_params=params(24),
        cost_estimate=pl.CostEstimate(
            flops=2 * rows * WIDTH * 3 * HW, bytes_accessed=14_000_000, transcendentals=0
        ),
        name="temporal_attention",
    )(scalars, x, w, w, w)


def encoded_kernel(scalars, *refs):
    count = len(CHUNKS)
    t_refs, m_refs = refs[:count], refs[count : 2 * count]
    w_ref, o_ref, rows_ref = refs[2 * count :]

    @pl.when(pl.program_id(0) == 0)
    def _():
        move = reorder(False)
        for n, off, t_ref in zip(CHUNKS, OFFSETS, t_refs):
            for b in range(n):
                block = t_ref[b * 16 : b * 16 + 16].reshape(64, HW)
                moved = jnp.dot(move, block, preferred_element_type=F32).astype(BF)
                for f in range(4):
                    lo = (off + b) * 16
                    rows_ref[f, lo : lo + 16, :] = moved[f * 16 : f * 16 + 16]

    first, limit = scalars[0], scalars[1]
    for f in range(4):
        valid = (first + f < limit).astype(F32)
        branch = jnp.dot(rows_ref[f], w_ref[...], preferred_element_type=F32)
        for n, off, m_ref in zip(CHUNKS, OFFSETS, m_refs):
            rows = slice(off * 16, (off + n) * 16)
            o_ref[f, rows, :] = (m_ref[f].astype(F32) + valid * branch[rows]).astype(BF)


def encoded_rows(scalars, temporals, middles, w):
    columns = 512
    return pl.pallas_call(
        encoded_kernel,
        grid=(WIDTH // columns,),
        in_specs=[pl.BlockSpec(memory_space=pltpu.SMEM)]
        + [pl.BlockSpec((16 * n, 4, HW), lambda j: (0, 0, 0)) for n in CHUNKS]
        + [pl.BlockSpec((4, 16 * n, columns), lambda j: (0, 0, j)) for n in CHUNKS]
        + [pl.BlockSpec((HW, columns), lambda j: (0, j))],
        out_specs=pl.BlockSpec((4, 144, columns), lambda j: (0, 0, j)),
        out_shape=jax.ShapeDtypeStruct((4, 144, WIDTH), BF),
        scratch_shapes=[pltpu.VMEM((4, 144, HW), BF)],
        compiler_params=params(24),
        cost_estimate=pl.CostEstimate(
            flops=8 * 144 * HW * WIDTH, bytes_accessed=8_000_000, transcendentals=0
        ),
        name="encoded_rows",
    )(scalars, *temporals, *middles, w)


def along_z(x, distance):
    pairs = [(i, (i + 2 * distance) % 8) for i in range(8)]
    return lax.ppermute(x, "space", pairs)


def over_tm(x):
    return lax.all_to_all(x, "tm", split_axis=0, concat_axis=0, tiled=True)


def per_device(video, frame_count, qkv_space, out_space, qkv_time, out_time):
    first = lax.axis_index("tm") * video.shape[0]
    z = lax.axis_index("space") // 2
    scalars = jnp.stack([first, frame_count[0], z]).astype(jnp.int32)

    frame = lax.all_to_all(
        video, "space", split_axis=0, concat_axis=0, axis_index_groups=Z_GROUPS, tiled=True
    )
    kv_own, norm1 = keys_values(scalars, frame.reshape(4 * 144, WIDTH), qkv_space)
    kv_other = lax.ppermute(kv_own, "space", SWAP)
    q = queries(norm1, qkv_space).reshape(4, 144, HW)
    back = {}
    for d in (2, 1, 3, 0):
        o = spatial_attention(scalars, q, kv_own, kv_other, d)
        back[d] = along_z(o, d) if d else o
    middle, send = middle_rows(scalars, [back[d] for d in range(4)], video, out_space)
    rows = over_tm(send.reshape(TM, 9, 4, WIDTH))
    temporal = temporal_attention(scalars, rows, qkv_time, 9)
    temporal = over_tm(temporal).reshape(144, 4, HW)
    return encoded_rows(scalars, [temporal], [middle], out_time)


def solution(mesh):
    return jax.shard_map(
        per_device,
        mesh=mesh,
        in_specs=(P("tm", "space", None), P(), P(), P(), P(), P()),
        out_specs=P("tm", "space", None),
        check_vma=False,
    )
```

```python
import functools

import jax
import jax.numpy as jnp
from jax import lax
from jax.experimental import pallas as pl
from jax.experimental.pallas import tpu as pltpu
from jax.sharding import PartitionSpec as P

H = 16
HD = 64
WIDTH = 1536
HW = H * HD
TM = 16
QSCALE = 0.125 * 1.4426950408889634
CALLS = ((2,), (1, 3), (0,))
SWAP = [(i, i ^ 1) for i in range(8)]
Z_GROUPS = [[0, 2, 4, 6], [1, 3, 5, 7]]
BF = jnp.bfloat16
F32 = jnp.float32


def params(mebibytes):
    return pltpu.CompilerParams(vmem_limit_bytes=mebibytes * 1024 * 1024)


def normalise(wide):
    center = wide - jnp.mean(wide, axis=-1, keepdims=True)
    spread = jnp.mean(center * center, axis=-1, keepdims=True)
    return (center * lax.rsqrt(spread + 1e-06)).astype(BF)


def nt_dot(a, b):
    return lax.dot_general(a, b, (((1,), (1,)), ((), ())), preferred_element_type=F32)


def tn_dot(a, b):
    return lax.dot_general(a, b, (((0,), (0,)), ((), ())), preferred_element_type=F32)


def kv_kernel(scalars, x_ref, w_ref, kv_ref, norm_ref, wq_ref, wkv, sem):
    def fetch(j):
        cols = pl.ds(pl.multiple_of(j * 512, 128), 512)
        source = pl.ds(pl.multiple_of(j * 512 + HW, 128), 512)
        return pltpu.make_async_copy(w_ref.at[:, source], wkv.at[:, cols], sem.at[j])

    for j in range(4):
        fetch(j).start()
    for_queries = pltpu.make_async_copy(w_ref.at[:, :HW], wq_ref, sem.at[4])
    for_queries.start()

    def norm(i, carry):
        rows = pl.ds(pl.multiple_of(i * 96, 96), 96)
        norm_ref[rows, :] = normalise(x_ref[rows, :].astype(F32))
        return carry

    lax.fori_loop(0, x_ref.shape[0] // 96, norm, 0)

    def step(j, carry):
        fetch(j).wait()
        cols = pl.ds(pl.multiple_of(j * 512, 128), 512)
        y = jnp.dot(norm_ref[...], wkv[:, cols], preferred_element_type=F32)
        kv_ref[:, cols] = y.astype(BF)
        return carry

    lax.fori_loop(0, 4, step, 0)
    for_queries.wait()


def keys_values(scalars, x, w):
    rows = x.shape[0]
    whole = pl.BlockSpec(memory_space=pltpu.VMEM)
    return pl.pallas_call(
        kv_kernel,
        in_specs=[
            pl.BlockSpec(memory_space=pltpu.SMEM),
            whole,
            pl.BlockSpec(memory_space=pltpu.HBM),
        ],
        out_specs=[whole, whole, whole],
        out_shape=[
            jax.ShapeDtypeStruct((rows, 2 * HW), BF),
            jax.ShapeDtypeStruct((rows, WIDTH), BF),
            jax.ShapeDtypeStruct((WIDTH, HW), BF),
        ],
        scratch_shapes=[pltpu.VMEM((WIDTH, 2 * HW), BF), pltpu.SemaphoreType.DMA((5,))],
        compiler_params=params(24),
        cost_estimate=pl.CostEstimate(
            flops=2 * rows * WIDTH * 2 * HW, bytes_accessed=12_000_000, transcendentals=0
        ),
        name="keys_values",
    )(scalars, x, pltpu.with_memory_space_constraint(w, pltpu.HBM))


def q_kernel(norm_ref, w_ref, q_ref):
    def step(j, carry):
        cols = pl.ds(pl.multiple_of(j * 512, 128), 512)
        y = jnp.dot(norm_ref[...], w_ref[:, cols], preferred_element_type=F32)
        q_ref[:, cols] = (y * QSCALE).astype(BF)
        return carry

    lax.fori_loop(0, 2, step, 0)


def queries(norm, w):
    rows = norm.shape[0]
    whole = pl.BlockSpec(memory_space=pltpu.VMEM)
    return pl.pallas_call(
        q_kernel,
        in_specs=[whole, whole],
        out_specs=whole,
        out_shape=jax.ShapeDtypeStruct((rows, HW), BF),
        compiler_params=params(16),
        cost_estimate=pl.CostEstimate(
            flops=2 * rows * WIDTH * HW, bytes_accessed=6_000_000, transcendentals=0
        ),
        name="queries",
    )(norm, w)


def spatial_kernel(distances, scalars, q_ref, a_ref, b_ref, *refs):
    count = len(distances)
    o_refs, (keys, values, s_a, s_b, m_a, m_b) = refs[:count], refs[count:]
    half, pairs, rows = a_ref.shape[0], H // 2, o_refs[0].shape[0]
    width = keys.shape[0]
    groups = pairs // width
    owners = [lax.rem(scalars[2] + d, 4) for d in distances]
    low = lax.broadcasted_iota(jnp.int32, (rows, 128), 1) < HD
    zero = jnp.zeros((rows, 128), BF)
    for e in range(width):
        values[e, :, 128:] = jnp.ones((2 * half, 128), BF)

    def columns(pair):
        if isinstance(pair, int):
            return slice(pair * 128, pair * 128 + 128)
        return pl.ds(pl.multiple_of(pair * 128, 128), 128)

    def load(pair, held, e):
        held[e, :half, :128] = a_ref[:, columns(pair)]
        held[e, half:, :128] = b_ref[:, columns(pair)]

    def score(group, e, c, head, s_ref, m_ref):
        slot = (e * count + c) * 2 + head
        q = q_ref[owners[c], :, columns(width * group + e)]
        q = jnp.where(low, q, zero) if head == 0 else jnp.where(low, zero, q)
        s = nt_dot(q, keys[e])
        s_ref[slot] = s
        m_ref[slot] = jnp.broadcast_to(jnp.max(s, axis=-1, keepdims=True), (rows, 128))

    def weigh(e, c, head, s_ref, m_ref):
        slot = (e * count + c) * 2 + head
        p = jnp.exp2(s_ref[slot] - m_ref[slot, :, :1]).astype(BF)
        o = jnp.dot(p, values[e], preferred_element_type=F32)
        return o[:, :128] / o[:, 128:]

    def phase(group, later, now, after):
        for e in range(width):
            load(width * group + e + pairs, values, e)
            if later is not None:
                load(width * later + e, keys, e)
        for e in range(width):
            for c in range(count):
                out = []
                for head in range(2):
                    if later is not None:
                        score(later, e, c, head, *after)
                    out.append(weigh(e, c, head, *now))
                o_refs[c][:, columns(width * group + e)] = jnp.where(low, out[0], out[1]).astype(BF)

    first, second = (s_a, m_a), (s_b, m_b)
    for e in range(width):
        load(e, keys, e)
        for c in range(count):
            for head in range(2):
                score(0, e, c, head, *first)

    def step(i, carry):
        phase(2 * i, 2 * i + 1, first, second)
        phase(2 * i + 1, 2 * i + 2, second, first)
        return carry

    lax.fori_loop(0, groups // 2 - 1, step, 0)
    phase(groups - 2, groups - 1, first, second)
    phase(groups - 1, None, second, first)


def spatial_attention(scalars, q, kv_a, kv_b, distances):
    rows, total, count = q.shape[1], 2 * kv_a.shape[0], len(distances)
    width = 4 // count
    heads = 2 * width * count
    whole = pl.BlockSpec(memory_space=pltpu.VMEM)
    return pl.pallas_call(
        functools.partial(spatial_kernel, distances),
        in_specs=[pl.BlockSpec(memory_space=pltpu.SMEM), whole, whole, whole],
        out_specs=[whole] * count,
        out_shape=[jax.ShapeDtypeStruct((rows, HW), BF)] * count,
        scratch_shapes=[pltpu.VMEM((width, total, 128), BF), pltpu.VMEM((width, total, 256), BF)]
        + [pltpu.VMEM((heads, rows, total), F32)] * 2
        + [pltpu.VMEM((heads, rows, 128), F32)] * 2,
        compiler_params=params(24),
        cost_estimate=pl.CostEstimate(
            flops=20 * count * rows * total * HW,
            bytes_accessed=6_000_000,
            transcendentals=count * rows * total * H,
        ),
        name="spatial_attention",
    )(scalars, q, kv_a, kv_b)


def reorder(to_patch_major):
    row = lax.broadcasted_iota(jnp.int32, (64, 64), 0)
    col = lax.broadcasted_iota(jnp.int32, (64, 64), 1)
    if to_patch_major:
        return (col == (row % 4) * 16 + row // 4).astype(BF)
    return (col == (row % 16) * 4 + row // 16).astype(BF)


def middle_kernel(scalars, *refs):
    s_refs, (x_ref, w_ref, middle_ref, send_ref, norm) = refs[:4], refs[4:]
    first, limit, z = scalars[0], scalars[1], scalars[2]
    for d in range(4):
        f = lax.rem(z + 4 - d, 4)
        valid = (first + f < limit).astype(F32)
        branch = jnp.dot(s_refs[d][...], w_ref[...], preferred_element_type=F32)
        middle = (x_ref[f].astype(F32) + valid * branch).astype(BF)
        middle_ref[f] = middle
        norm[f] = normalise(middle.astype(F32))
    move = reorder(True)
    for b in range(9):
        rows = slice(b * 16, b * 16 + 16)
        block = jnp.concatenate([norm[f, rows, :] for f in range(4)], axis=0)
        moved = jnp.dot(move, block, preferred_element_type=F32).astype(BF)
        send_ref[rows] = moved.reshape(16, 4, WIDTH)


def middle_rows(scalars, blocks, video, w):
    whole = pl.BlockSpec(memory_space=pltpu.VMEM)
    return pl.pallas_call(
        middle_kernel,
        in_specs=[pl.BlockSpec(memory_space=pltpu.SMEM)] + [whole] * 6,
        out_specs=[whole, whole],
        out_shape=[
            jax.ShapeDtypeStruct((4, 144, WIDTH), BF),
            jax.ShapeDtypeStruct((144, 4, WIDTH), BF),
        ],
        scratch_shapes=[pltpu.VMEM((4, 144, WIDTH), BF)],
        compiler_params=params(24),
        cost_estimate=pl.CostEstimate(
            flops=8 * 144 * HW * WIDTH, bytes_accessed=8_000_000, transcendentals=0
        ),
        name="middle_rows",
    )(scalars, *blocks, video, w)


def temporal_kernel(n, scalars, x_ref, w_ref, o_ref, rows_ref):
    for i in range(n):
        rows_ref[64 * i : 64 * i + 64, :] = x_ref[:, i].reshape(64, WIDTH)
    limit = scalars[1]
    head_row = lax.broadcasted_iota(jnp.int32, (256, 256), 0) // HD
    head_col = lax.broadcasted_iota(jnp.int32, (256, 256), 1) // HD
    same = head_row == head_col
    zero = jnp.zeros((256, 256), BF)
    key_valid = lax.broadcasted_iota(jnp.int32, (4, 64, 64), 1) < limit

    def step(g, carry):
        def project(part):
            cols = pl.ds(pl.multiple_of(part * HW + g * 256, 128), 256)
            return jnp.dot(rows_ref[...], w_ref[:, cols], preferred_element_type=F32)

        q = (project(0) * QSCALE).astype(BF)
        k = project(1).astype(BF)
        v = project(2).astype(BF)
        scores, weights = [], []
        for i in range(n):
            rows = slice(64 * i, 64 * i + 64)
            k4 = jnp.where(same, jnp.concatenate([k[rows]] * 4, axis=0), zero)
            scores.append(nt_dot(k4, q[rows]).reshape(4, 64, 64))
        for i in range(n):
            s = jnp.where(key_valid, scores[i], -1e30)
            p = jnp.exp2(s - jnp.max(s, axis=1, keepdims=True))
            p = p / jnp.sum(p, axis=1, keepdims=True)
            weights.append(p.reshape(256, 64).astype(BF))
        cols = pl.ds(pl.multiple_of(g * 256, 128), 256)
        for i in range(n):
            rows = slice(64 * i, 64 * i + 64)
            v4 = jnp.where(same, jnp.concatenate([v[rows]] * 4, axis=0), zero)
            o_ref[:, i, :, cols] = tn_dot(weights[i], v4).astype(BF).reshape(16, 4, 256)
        return carry

    lax.fori_loop(0, 4, step, 0)


def temporal_attention(scalars, x, w, n):
    rows = 64 * n
    whole = pl.BlockSpec(memory_space=pltpu.VMEM)
    return pl.pallas_call(
        functools.partial(temporal_kernel, n),
        in_specs=[pl.BlockSpec(memory_space=pltpu.SMEM), whole, whole],
        out_specs=whole,
        out_shape=jax.ShapeDtypeStruct((TM, n, 4, HW), BF),
        scratch_shapes=[pltpu.VMEM((rows, WIDTH), BF)],
        compiler_params=params(24),
        cost_estimate=pl.CostEstimate(
            flops=2 * rows * WIDTH * 3 * HW, bytes_accessed=14_000_000, transcendentals=0
        ),
        name="temporal_attention",
    )(scalars, x, w)


def encoded_kernel(scalars, t_ref, m_ref, w_ref, o_ref, rows_ref, held, sem):
    move = reorder(False)
    for b in range(9):
        block = t_ref[b * 16 : b * 16 + 16].reshape(64, HW)
        moved = jnp.dot(move, block, preferred_element_type=F32).astype(BF)
        for f in range(4):
            lo = f * 144 + b * 16
            rows_ref[lo : lo + 16, :] = moved[f * 16 : f * 16 + 16]
    first, limit = scalars[0], scalars[1]

    def leave(j):
        cols = pl.ds(pl.multiple_of(j * 512, 128), 512)
        return pltpu.make_async_copy(held.at[:, :, cols], o_ref.at[:, :, cols], sem.at[j])

    def project(j, carry):
        cols = pl.ds(pl.multiple_of(j * 512, 128), 512)
        branch = jnp.dot(rows_ref[...], w_ref[:, cols], preferred_element_type=F32)
        for f in range(4):
            valid = (first + f < limit).astype(F32)
            own = branch[f * 144 : (f + 1) * 144]
            held[f, :, cols] = (m_ref[f, :, cols].astype(F32) + valid * own).astype(BF)
        leave(j).start()
        return carry

    lax.fori_loop(0, 3, project, 0)
    for j in range(3):
        leave(j).wait()


def encoded_rows(scalars, temporal, middle, w):
    whole = pl.BlockSpec(memory_space=pltpu.VMEM)
    return pl.pallas_call(
        encoded_kernel,
        in_specs=[pl.BlockSpec(memory_space=pltpu.SMEM), whole, whole, whole],
        out_specs=pl.BlockSpec(memory_space=pltpu.HBM),
        out_shape=jax.ShapeDtypeStruct((4, 144, WIDTH), BF),
        scratch_shapes=[
            pltpu.VMEM((4 * 144, HW), BF),
            pltpu.VMEM((4, 144, WIDTH), BF),
            pltpu.SemaphoreType.DMA((3,)),
        ],
        compiler_params=params(24),
        cost_estimate=pl.CostEstimate(
            flops=8 * 144 * HW * WIDTH, bytes_accessed=8_000_000, transcendentals=0
        ),
        name="encoded_rows",
    )(scalars, temporal, middle, w)


def along_z(x, distance):
    pairs = [(i, (i + 2 * distance) % 8) for i in range(8)]
    return lax.ppermute(x, "space", pairs)


def over_tm(x):
    return lax.all_to_all(x, "tm", split_axis=0, concat_axis=0, tiled=True)


def per_device(video, frame_count, qkv_space, out_space, qkv_time, out_time):
    first = lax.axis_index("tm") * video.shape[0]
    z = lax.axis_index("space") // 2
    scalars = jnp.stack([first, frame_count[0], z]).astype(jnp.int32)

    frame = lax.all_to_all(
        video, "space", split_axis=0, concat_axis=0, axis_index_groups=Z_GROUPS, tiled=True
    )
    kv_own, norm1, w_q = keys_values(scalars, frame.reshape(4 * 144, WIDTH), qkv_space)
    kv_other = lax.ppermute(kv_own, "space", SWAP)
    q = queries(norm1, w_q).reshape(4, 144, HW)
    back = {}
    for distances in CALLS:
        results = spatial_attention(scalars, q, kv_own, kv_other, distances)
        for d, o in zip(distances, results):
            back[d] = along_z(o, d) if d else o
    middle, send = middle_rows(scalars, [back[d] for d in range(4)], video, out_space)
    rows = over_tm(send.reshape(TM, 9, 4, WIDTH))
    temporal = temporal_attention(scalars, rows, qkv_time, 9)
    temporal = over_tm(temporal).reshape(144, 4, HW)
    return encoded_rows(scalars, temporal, middle, out_time)


def solution(mesh):
    return jax.shard_map(
        per_device,
        mesh=mesh,
        in_specs=(P("tm", "space", None), P(), P(), P(), P(), P()),
        out_specs=P("tm", "space", None),
        check_vma=False,
    )
```

```python
import functools

import jax
import jax.numpy as jnp
from jax import lax
from jax.experimental import pallas as pl
from jax.experimental.pallas import tpu as pltpu
from jax.sharding import PartitionSpec as P

H = 16
HD = 64
WIDTH = 1536
HW = H * HD
TM = 16
QSCALE = 0.125 * 1.4426950408889634
CALLS = ((1, 3), (2,))
LATE = 2
SWAP = [(i, i ^ 1) for i in range(8)]
Z_GROUPS = [[0, 2, 4, 6], [1, 3, 5, 7]]
BF = jnp.bfloat16
F32 = jnp.float32


def params(mebibytes):
    return pltpu.CompilerParams(vmem_limit_bytes=mebibytes * 1024 * 1024)


def normalise(wide):
    center = wide - jnp.mean(wide, axis=-1, keepdims=True)
    spread = jnp.mean(center * center, axis=-1, keepdims=True)
    return (center * lax.rsqrt(spread + 1e-06)).astype(BF)


def nt_dot(a, b):
    return lax.dot_general(a, b, (((1,), (1,)), ((), ())), preferred_element_type=F32)


def tn_dot(a, b):
    return lax.dot_general(a, b, (((0,), (0,)), ((), ())), preferred_element_type=F32)


def block(j):
    return pl.ds(pl.multiple_of(j * 512, 128), 512)


def own_kernel(scalars, video_ref, w_ref, kv_ref, q_ref, x_ref, norm_ref, held, sem):
    mine = pltpu.make_async_copy(video_ref.at[scalars[2]], x_ref, sem.at[6])
    mine.start()

    def fetch(j):
        return pltpu.make_async_copy(w_ref.at[:, block(j)], held.at[:, block(j)], sem.at[j])

    for j in (2, 3, 4, 5, 0, 1):
        fetch(j).start()
    mine.wait()

    def norm(i, carry):
        rows = pl.ds(pl.multiple_of(i * 48, 48), 48)
        norm_ref[rows, :] = normalise(x_ref[rows, :].astype(F32))
        return carry

    lax.fori_loop(0, 3, norm, 0)

    def key_value(j, carry):
        fetch(j).wait()
        y = jnp.dot(norm_ref[...], held[:, block(j)], preferred_element_type=F32)
        kv_ref[:, block(j - 2)] = y.astype(BF)
        return carry

    def query(j, carry):
        fetch(j).wait()
        y = jnp.dot(norm_ref[...], held[:, block(j)], preferred_element_type=F32)
        q_ref[0, :, block(j)] = (y * QSCALE).astype(BF)
        return carry

    lax.fori_loop(2, 6, key_value, 0)
    lax.fori_loop(0, 2, query, 0)


def own_block(scalars, video, w):
    rows = video.shape[1]
    whole = pl.BlockSpec(memory_space=pltpu.VMEM)
    far = pl.BlockSpec(memory_space=pltpu.HBM)
    return pl.pallas_call(
        own_kernel,
        in_specs=[pl.BlockSpec(memory_space=pltpu.SMEM), far, far],
        out_specs=[whole, whole],
        out_shape=[
            jax.ShapeDtypeStruct((rows, 2 * HW), BF),
            jax.ShapeDtypeStruct((1, rows, HW), BF),
        ],
        scratch_shapes=[
            pltpu.VMEM((rows, WIDTH), BF),
            pltpu.VMEM((rows, WIDTH), BF),
            pltpu.VMEM((WIDTH, 3 * HW), BF),
            pltpu.SemaphoreType.DMA((7,)),
        ],
        compiler_params=params(24),
        cost_estimate=pl.CostEstimate(
            flops=2 * rows * WIDTH * 3 * HW, bytes_accessed=12_000_000, transcendentals=0
        ),
        name="own_block",
    )(
        scalars,
        pltpu.with_memory_space_constraint(video, pltpu.HBM),
        pltpu.with_memory_space_constraint(w, pltpu.HBM),
    )


def kv_kernel(scalars, x_ref, w_ref, kv_ref, norm_ref, wq_ref, wkv, sem):
    def fetch(j):
        source = pl.ds(pl.multiple_of(j * 512 + HW, 128), 512)
        return pltpu.make_async_copy(w_ref.at[:, source], wkv.at[:, block(j)], sem.at[j])

    for j in range(4):
        fetch(j).start()
    for_queries = pltpu.make_async_copy(w_ref.at[:, :HW], wq_ref, sem.at[4])
    for_queries.start()
    for d in range(1, 4):
        other = lax.rem(scalars[2] + d, 4)

        def norm(i, carry):
            lo = pl.multiple_of(i * 48, 48)
            wide = x_ref[other, pl.ds(lo, 48), :].astype(F32)
            norm_ref[pl.ds((d - 1) * 144 + lo, 48), :] = normalise(wide)
            return carry

        lax.fori_loop(0, 3, norm, 0, unroll=True)

    def step(j, carry):
        fetch(j).wait()
        y = jnp.dot(norm_ref[...], wkv[:, block(j)], preferred_element_type=F32)
        kv_ref[:, block(j)] = y.astype(BF)
        return carry

    lax.fori_loop(0, 4, step, 0)
    for_queries.wait()


def keys_values(scalars, x, w):
    rows = 3 * x.shape[1]
    whole = pl.BlockSpec(memory_space=pltpu.VMEM)
    return pl.pallas_call(
        kv_kernel,
        in_specs=[
            pl.BlockSpec(memory_space=pltpu.SMEM),
            whole,
            pl.BlockSpec(memory_space=pltpu.HBM),
        ],
        out_specs=[whole, whole, whole],
        out_shape=[
            jax.ShapeDtypeStruct((rows, 2 * HW), BF),
            jax.ShapeDtypeStruct((rows, WIDTH), BF),
            jax.ShapeDtypeStruct((WIDTH, HW), BF),
        ],
        scratch_shapes=[pltpu.VMEM((WIDTH, 2 * HW), BF), pltpu.SemaphoreType.DMA((5,))],
        compiler_params=params(24),
        cost_estimate=pl.CostEstimate(
            flops=2 * rows * WIDTH * 2 * HW, bytes_accessed=12_000_000, transcendentals=0
        ),
        name="keys_values",
    )(scalars, x, pltpu.with_memory_space_constraint(w, pltpu.HBM))


def q_kernel(norm_ref, w_ref, q_ref):
    def step(j, carry):
        y = jnp.dot(norm_ref[...], w_ref[:, block(j)], preferred_element_type=F32)
        q = (y * QSCALE).astype(BF)
        for d in range(3):
            q_ref[d, :, block(j)] = q[d * 144 : (d + 1) * 144]
        return carry

    lax.fori_loop(0, 2, step, 0)


def queries(norm, w):
    rows = norm.shape[0]
    whole = pl.BlockSpec(memory_space=pltpu.VMEM)
    return pl.pallas_call(
        q_kernel,
        in_specs=[whole, whole],
        out_specs=whole,
        out_shape=jax.ShapeDtypeStruct((3, 144, HW), BF),
        compiler_params=params(16),
        cost_estimate=pl.CostEstimate(
            flops=2 * rows * WIDTH * HW, bytes_accessed=6_000_000, transcendentals=0
        ),
        name="queries",
    )(norm, w)


def spatial_kernel(which, q_ref, *refs):
    count = len(which)
    kv_refs, o_refs = refs[: -count - 6], refs[-count - 6 : -6]
    keys, values, s_a, s_b, m_a, m_b = refs[-6:]
    pairs, rows = H // 2, o_refs[0].shape[0]
    width = keys.shape[0]
    groups = pairs // width
    low = lax.broadcasted_iota(jnp.int32, (rows, 128), 1) < HD
    zero = jnp.zeros((rows, 128), BF)
    for e in range(width):
        values[e, :, 128:] = jnp.ones((values.shape[1], 128), BF)

    def columns(pair):
        if isinstance(pair, int):
            return slice(pair * 128, pair * 128 + 128)
        return pl.ds(pl.multiple_of(pair * 128, 128), 128)

    def load(pair, held, e):
        lo = 0
        for ref in kv_refs:
            held[e, lo : lo + ref.shape[0], :128] = ref[:, columns(pair)]
            lo += ref.shape[0]

    def score(group, e, c, head, s_ref, m_ref):
        slot = (e * count + c) * 2 + head
        q = q_ref[which[c], :, columns(width * group + e)]
        q = jnp.where(low, q, zero) if head == 0 else jnp.where(low, zero, q)
        s = nt_dot(q, keys[e])
        s_ref[slot] = s
        m_ref[slot] = jnp.broadcast_to(jnp.max(s, axis=-1, keepdims=True), (rows, 128))

    def weigh(e, c, head, s_ref, m_ref):
        slot = (e * count + c) * 2 + head
        p = jnp.exp2(s_ref[slot] - m_ref[slot, :, :1]).astype(BF)
        o = jnp.dot(p, values[e], preferred_element_type=F32)
        return o[:, :128] / o[:, 128:]

    def phase(group, later, now, after):
        for e in range(width):
            load(width * group + e + pairs, values, e)
            if later is not None:
                load(width * later + e, keys, e)
        for e in range(width):
            for c in range(count):
                out = []
                for head in range(2):
                    if later is not None:
                        score(later, e, c, head, *after)
                    out.append(weigh(e, c, head, *now))
                o_refs[c][:, columns(width * group + e)] = jnp.where(low, out[0], out[1]).astype(BF)

    first, second = (s_a, m_a), (s_b, m_b)
    for e in range(width):
        load(e, keys, e)
        for c in range(count):
            for head in range(2):
                score(0, e, c, head, *first)

    def step(i, carry):
        phase(2 * i, 2 * i + 1, first, second)
        phase(2 * i + 1, 2 * i + 2, second, first)
        return carry

    lax.fori_loop(0, groups // 2 - 1, step, 0)
    phase(groups - 2, groups - 1, first, second)
    phase(groups - 1, None, second, first)


def spatial_attention(q, kvs, which):
    rows, total, count = q.shape[1], sum(kv.shape[0] for kv in kvs), len(which)
    width = 4 // count
    heads = 2 * width * count
    whole = pl.BlockSpec(memory_space=pltpu.VMEM)
    return pl.pallas_call(
        functools.partial(spatial_kernel, which),
        in_specs=[whole] * (1 + len(kvs)),
        out_specs=[whole] * count,
        out_shape=[jax.ShapeDtypeStruct((rows, HW), BF)] * count,
        scratch_shapes=[pltpu.VMEM((width, total, 128), BF), pltpu.VMEM((width, total, 256), BF)]
        + [pltpu.VMEM((heads, rows, total), F32)] * 2
        + [pltpu.VMEM((heads, rows, 128), F32)] * 2,
        compiler_params=params(24),
        cost_estimate=pl.CostEstimate(
            flops=count * rows * total * HW,
            bytes_accessed=1_000_000,
            transcendentals=0,
        ),
        name="spatial_attention",
    )(q, *kvs)


def reorder(to_patch_major):
    row = lax.broadcasted_iota(jnp.int32, (64, 64), 0)
    col = lax.broadcasted_iota(jnp.int32, (64, 64), 1)
    if to_patch_major:
        return (col == (row % 4) * 16 + row // 4).astype(BF)
    return (col == (row % 16) * 4 + row // 16).astype(BF)


def home(scalars, d):
    return lax.rem(scalars[2] + 4 - d, 4)


def middle_of(scalars, f, s_ref, x_ref, w_ref):
    valid = (scalars[0] + f < scalars[1]).astype(F32)
    branch = jnp.dot(s_ref[...], w_ref[...], preferred_element_type=F32)
    return (x_ref[f].astype(F32) + valid * branch).astype(BF)


def early_kernel(distances, scalars, *refs):
    s_refs, (x_ref, w_ref, middle_ref, norm_ref) = refs[:-4], refs[-4:]
    for d, s_ref in zip(distances, s_refs):
        f = home(scalars, d)
        middle = middle_of(scalars, f, s_ref, x_ref, w_ref)
        middle_ref[f] = middle
        norm_ref[f] = normalise(middle.astype(F32))


def early_rows(scalars, blocks, distances, video, w):
    whole = pl.BlockSpec(memory_space=pltpu.VMEM)
    return pl.pallas_call(
        functools.partial(early_kernel, distances),
        in_specs=[pl.BlockSpec(memory_space=pltpu.SMEM)] + [whole] * (2 + len(blocks)),
        out_specs=[whole, whole],
        out_shape=[jax.ShapeDtypeStruct((4, 144, WIDTH), BF)] * 2,
        compiler_params=params(16),
        cost_estimate=pl.CostEstimate(
            flops=2 * len(blocks) * 144 * HW * WIDTH, bytes_accessed=8_000_000, transcendentals=0
        ),
        name="early_rows",
    )(scalars, *blocks, video, w)


def late_kernel(distance, scalars, s_ref, norm_ref, x_ref, w_ref, middle_ref, send_ref, late):
    last = home(scalars, distance)
    middle = middle_of(scalars, last, s_ref, x_ref, w_ref)
    middle_ref[...] = middle
    late[...] = normalise(middle.astype(F32))
    move = reorder(True)
    for b in range(9):
        rows = slice(b * 16, b * 16 + 16)
        parts = [jnp.where(last == f, late[rows, :], norm_ref[f, rows, :]) for f in range(4)]
        moved = jnp.dot(move, jnp.concatenate(parts, axis=0), preferred_element_type=F32)
        send_ref[rows] = moved.astype(BF).reshape(16, 4, WIDTH)


def late_rows(scalars, spatial, norm, distance, video, w):
    whole = pl.BlockSpec(memory_space=pltpu.VMEM)
    return pl.pallas_call(
        functools.partial(late_kernel, distance),
        in_specs=[pl.BlockSpec(memory_space=pltpu.SMEM)] + [whole] * 4,
        out_specs=[whole, whole],
        out_shape=[
            jax.ShapeDtypeStruct((144, WIDTH), BF),
            jax.ShapeDtypeStruct((144, 4, WIDTH), BF),
        ],
        scratch_shapes=[pltpu.VMEM((144, WIDTH), BF)],
        compiler_params=params(16),
        cost_estimate=pl.CostEstimate(
            flops=2 * 144 * HW * WIDTH, bytes_accessed=8_000_000, transcendentals=0
        ),
        name="late_rows",
    )(scalars, spatial, norm, video, w)


def temporal_kernel(n, scalars, x_ref, w_ref, o_ref, rows_ref):
    for i in range(n):
        rows_ref[64 * i : 64 * i + 64, :] = x_ref[:, i].reshape(64, WIDTH)
    limit = scalars[1]
    head_row = lax.broadcasted_iota(jnp.int32, (256, 256), 0) // HD
    head_col = lax.broadcasted_iota(jnp.int32, (256, 256), 1) // HD
    same = head_row == head_col
    zero = jnp.zeros((256, 256), BF)
    key_valid = lax.broadcasted_iota(jnp.int32, (4, 64, 64), 1) < limit

    def step(g, carry):
        def project(part):
            cols = pl.ds(pl.multiple_of(part * HW + g * 256, 128), 256)
            return jnp.dot(rows_ref[...], w_ref[:, cols], preferred_element_type=F32)

        q = (project(0) * QSCALE).astype(BF)
        k = project(1).astype(BF)
        v = project(2).astype(BF)
        scores, weights = [], []
        for i in range(n):
            rows = slice(64 * i, 64 * i + 64)
            k4 = jnp.where(same, jnp.concatenate([k[rows]] * 4, axis=0), zero)
            scores.append(nt_dot(k4, q[rows]).reshape(4, 64, 64))
        for i in range(n):
            s = jnp.where(key_valid, scores[i], -1e30)
            p = jnp.exp2(s - jnp.max(s, axis=1, keepdims=True))
            p = p / jnp.sum(p, axis=1, keepdims=True)
            weights.append(p.reshape(256, 64).astype(BF))
        cols = pl.ds(pl.multiple_of(g * 256, 128), 256)
        for i in range(n):
            rows = slice(64 * i, 64 * i + 64)
            v4 = jnp.where(same, jnp.concatenate([v[rows]] * 4, axis=0), zero)
            o_ref[:, i, :, cols] = tn_dot(weights[i], v4).astype(BF).reshape(16, 4, 256)
        return carry

    lax.fori_loop(0, 4, step, 0)


def temporal_attention(scalars, x, w, n):
    rows = 64 * n
    whole = pl.BlockSpec(memory_space=pltpu.VMEM)
    return pl.pallas_call(
        functools.partial(temporal_kernel, n),
        in_specs=[pl.BlockSpec(memory_space=pltpu.SMEM), whole, whole],
        out_specs=whole,
        out_shape=jax.ShapeDtypeStruct((TM, n, 4, HW), BF),
        scratch_shapes=[pltpu.VMEM((rows, WIDTH), BF)],
        compiler_params=params(24),
        cost_estimate=pl.CostEstimate(
            flops=2 * rows * WIDTH * 3 * HW, bytes_accessed=14_000_000, transcendentals=0
        ),
        name="temporal_attention",
    )(scalars, x, w)


def encoded_kernel(distance, scalars, t_ref, m_ref, late_ref, w_ref, o_ref, rows_ref, held, sem):
    last = home(scalars, distance)
    move = reorder(False)
    for b in range(9):
        block = t_ref[b * 16 : b * 16 + 16].reshape(64, HW)
        moved = jnp.dot(move, block, preferred_element_type=F32).astype(BF)
        for f in range(4):
            lo = f * 144 + b * 16
            rows_ref[lo : lo + 16, :] = moved[f * 16 : f * 16 + 16]
    first, limit = scalars[0], scalars[1]

    def leave(j):
        cols = pl.ds(pl.multiple_of(j * 512, 128), 512)
        return pltpu.make_async_copy(held.at[:, :, cols], o_ref.at[:, :, cols], sem.at[j])

    def project(j, carry):
        cols = pl.ds(pl.multiple_of(j * 512, 128), 512)
        branch = jnp.dot(rows_ref[...], w_ref[:, cols], preferred_element_type=F32)
        for f in range(4):
            valid = (first + f < limit).astype(F32)
            own = branch[f * 144 : (f + 1) * 144]
            middle = jnp.where(last == f, late_ref[:, cols], m_ref[f, :, cols])
            held[f, :, cols] = (middle.astype(F32) + valid * own).astype(BF)
        leave(j).start()
        return carry

    lax.fori_loop(0, 3, project, 0)
    for j in range(3):
        leave(j).wait()


def encoded_rows(scalars, temporal, middle, late, distance, w):
    whole = pl.BlockSpec(memory_space=pltpu.VMEM)
    return pl.pallas_call(
        functools.partial(encoded_kernel, distance),
        in_specs=[pl.BlockSpec(memory_space=pltpu.SMEM)] + [whole] * 4,
        out_specs=pl.BlockSpec(memory_space=pltpu.HBM),
        out_shape=jax.ShapeDtypeStruct((4, 144, WIDTH), BF),
        scratch_shapes=[
            pltpu.VMEM((4 * 144, HW), BF),
            pltpu.VMEM((4, 144, WIDTH), BF),
            pltpu.SemaphoreType.DMA((3,)),
        ],
        compiler_params=params(24),
        cost_estimate=pl.CostEstimate(
            flops=8 * 144 * HW * WIDTH, bytes_accessed=8_000_000, transcendentals=0
        ),
        name="encoded_rows",
    )(scalars, temporal, middle, late, w)


def along_z(x, distance):
    pairs = [(i, (i + 2 * distance) % 8) for i in range(8)]
    return lax.ppermute(x, "space", pairs)


def over_tm(x):
    return lax.all_to_all(x, "tm", split_axis=0, concat_axis=0, tiled=True)


def per_device(video, frame_count, qkv_space, out_space, qkv_time, out_time):
    first = lax.axis_index("tm") * video.shape[0]
    z = lax.axis_index("space") // 2
    scalars = jnp.stack([first, frame_count[0], z]).astype(jnp.int32)

    frame = lax.all_to_all(
        video, "space", split_axis=0, concat_axis=0, axis_index_groups=Z_GROUPS, tiled=True
    )
    kv_own, q_own = own_block(scalars, video, qkv_space)
    kv_own_other = lax.ppermute(kv_own, "space", SWAP)
    frame, kv_own, kv_own_other = lax.optimization_barrier((frame, kv_own, kv_own_other))
    kv_rest, norm1, w_q = keys_values(scalars, frame, qkv_space)
    kv_rest_other = lax.ppermute(kv_rest, "space", SWAP)
    q_rest = queries(norm1, w_q)
    kvs = (kv_rest, kv_own, kv_rest_other, kv_own_other)
    back = {}
    for distances in CALLS:
        results = spatial_attention(q_rest, kvs, [d - 1 for d in distances])
        q_rest, q_own, *results = lax.optimization_barrier((q_rest, q_own, *results))
        for d, o in zip(distances, results):
            back[d] = along_z(o, d)
    (back[0],) = spatial_attention(q_own, kvs, [0])
    early = tuple(d for d in (0, 1, 2, 3) if d != LATE)
    middle, norm2 = early_rows(scalars, [back[d] for d in early], early, video, out_space)
    late, send = late_rows(scalars, back[LATE], norm2, LATE, video, out_space)
    rows = over_tm(send.reshape(TM, 9, 4, WIDTH))
    temporal = temporal_attention(scalars, rows, qkv_time, 9)
    temporal = over_tm(temporal).reshape(144, 4, HW)
    return encoded_rows(scalars, temporal, middle, late, LATE, out_time)


def solution(mesh):
    return jax.shard_map(
        per_device,
        mesh=mesh,
        in_specs=(P("tm", "space", None), P(), P(), P(), P(), P()),
        out_specs=P("tm", "space", None),
        check_vma=False,
    )
```

```python
import functools

import jax
import jax.numpy as jnp
from jax import lax
from jax.experimental import pallas as pl
from jax.experimental.pallas import tpu as pltpu
from jax.sharding import PartitionSpec as P

H = 16
HD = 64
WIDTH = 1536
HW = H * HD
TM = 16
QSCALE = 0.125 * 1.4426950408889634
LATE = 2
SWAP = [(i, i ^ 1) for i in range(8)]
BF = jnp.bfloat16
F32 = jnp.float32


HEAVY = pl.CostEstimate(flops=20_000_000_000, bytes_accessed=1_000_000, transcendentals=0)
LIGHT = pl.CostEstimate(flops=100_000_000, bytes_accessed=1_000_000, transcendentals=0)


def params(mebibytes):
    return pltpu.CompilerParams(vmem_limit_bytes=mebibytes * 1024 * 1024)


def normalise(wide):
    center = wide - jnp.mean(wide, axis=-1, keepdims=True)
    spread = jnp.mean(center * center, axis=-1, keepdims=True)
    return (center * lax.rsqrt(spread + 1e-06)).astype(BF)


def nt_dot(a, b):
    return lax.dot_general(a, b, (((1,), (1,)), ((), ())), preferred_element_type=F32)


def tn_dot(a, b):
    return lax.dot_general(a, b, (((0,), (0,)), ((), ())), preferred_element_type=F32)


def block(j):
    return pl.ds(pl.multiple_of(j * 512, 128), 512)


def own_kernel(scalars, video_ref, w_ref, kv_ref, q_ref, x_ref, norm_ref, held, sem):
    mine = pltpu.make_async_copy(video_ref.at[scalars[2]], x_ref, sem.at[6])
    mine.start()

    def fetch(j):
        return pltpu.make_async_copy(w_ref.at[:, block(j)], held.at[:, block(j)], sem.at[j])

    for j in (2, 3, 4, 5, 0, 1):
        fetch(j).start()
    mine.wait()

    def norm(i, carry):
        rows = pl.ds(pl.multiple_of(i * 48, 48), 48)
        norm_ref[rows, :] = normalise(x_ref[rows, :].astype(F32))
        return carry

    lax.fori_loop(0, 3, norm, 0)

    def key_value(j, carry):
        fetch(j).wait()
        y = jnp.dot(norm_ref[...], held[:, block(j)], preferred_element_type=F32)
        kv_ref[:, block(j - 2)] = y.astype(BF)
        return carry

    def query(j, carry):
        fetch(j).wait()
        y = jnp.dot(norm_ref[...], held[:, block(j)], preferred_element_type=F32)
        q_ref[0, :, block(j)] = (y * QSCALE).astype(BF)
        return carry

    lax.fori_loop(2, 6, key_value, 0)
    lax.fori_loop(0, 2, query, 0)


def own_block(scalars, video, w):
    rows = video.shape[1]
    whole = pl.BlockSpec(memory_space=pltpu.VMEM)
    far = pl.BlockSpec(memory_space=pltpu.HBM)
    return pl.pallas_call(
        own_kernel,
        in_specs=[pl.BlockSpec(memory_space=pltpu.SMEM), far, far],
        out_specs=[whole, whole],
        out_shape=[
            jax.ShapeDtypeStruct((rows, 2 * HW), BF),
            jax.ShapeDtypeStruct((1, rows, HW), BF),
        ],
        scratch_shapes=[
            pltpu.VMEM((rows, WIDTH), BF),
            pltpu.VMEM((rows, WIDTH), BF),
            pltpu.VMEM((WIDTH, 3 * HW), BF),
            pltpu.SemaphoreType.DMA((7,)),
        ],
        compiler_params=params(24),
        cost_estimate=LIGHT,
        name="own_block",
    )(
        scalars,
        pltpu.with_memory_space_constraint(video, pltpu.HBM),
        pltpu.with_memory_space_constraint(w, pltpu.HBM),
    )


def near_kernel(count, *refs):
    x_refs, (w_ref, kv_ref, q_ref, norm_ref, held, sem) = refs[:count], refs[count:]

    def fetch(j):
        return pltpu.make_async_copy(w_ref.at[:, block(j)], held.at[:, block(j)], sem.at[j])

    for j in (2, 3, 4, 5, 0, 1):
        fetch(j).start()
    normalise_blocks(x_refs, norm_ref)

    def key_value(j, carry):
        fetch(j).wait()
        y = jnp.dot(norm_ref[...], held[:, block(j)], preferred_element_type=F32)
        kv_ref[:, block(j - 2)] = y.astype(BF)
        return carry

    def query(j, carry):
        fetch(j).wait()
        y = jnp.dot(norm_ref[...], held[:, block(j)], preferred_element_type=F32)
        q = (y * QSCALE).astype(BF)
        for b in range(count):
            q_ref[b, :, block(j)] = q[b * 144 : (b + 1) * 144]
        return carry

    lax.fori_loop(2, 6, key_value, 0)
    lax.fori_loop(0, 2, query, 0)


def normalise_blocks(x_refs, norm_ref):
    for b, x_ref in enumerate(x_refs):

        def norm(i, carry):
            lo = pl.multiple_of(i * 48, 48)
            norm_ref[pl.ds(b * 144 + lo, 48), :] = normalise(x_ref[pl.ds(lo, 48), :].astype(F32))
            return carry

        lax.fori_loop(0, 3, norm, 0, unroll=True)


def near_blocks(blocks, w):
    count, rows = len(blocks), 144 * len(blocks)
    whole = pl.BlockSpec(memory_space=pltpu.VMEM)
    return pl.pallas_call(
        functools.partial(near_kernel, count),
        in_specs=[whole] * count + [pl.BlockSpec(memory_space=pltpu.HBM)],
        out_specs=[whole, whole],
        out_shape=[
            jax.ShapeDtypeStruct((rows, 2 * HW), BF),
            jax.ShapeDtypeStruct((count, 144, HW), BF),
        ],
        scratch_shapes=[
            pltpu.VMEM((rows, WIDTH), BF),
            pltpu.VMEM((WIDTH, 3 * HW), BF),
            pltpu.SemaphoreType.DMA((6,)),
        ],
        compiler_params=params(24),
        cost_estimate=LIGHT,
        name="near_blocks",
    )(*blocks, pltpu.with_memory_space_constraint(w, pltpu.HBM))


def kv_kernel(x_ref, w_ref, kv_ref, norm_ref, wq_ref, wkv, sem):
    def fetch(j):
        source = pl.ds(pl.multiple_of(j * 512 + HW, 128), 512)
        return pltpu.make_async_copy(w_ref.at[:, source], wkv.at[:, block(j)], sem.at[j])

    for j in range(4):
        fetch(j).start()
    for_queries = pltpu.make_async_copy(w_ref.at[:, :HW], wq_ref, sem.at[4])
    for_queries.start()
    normalise_blocks([x_ref], norm_ref)

    def step(j, carry):
        fetch(j).wait()
        y = jnp.dot(norm_ref[...], wkv[:, block(j)], preferred_element_type=F32)
        kv_ref[:, block(j)] = y.astype(BF)
        return carry

    lax.fori_loop(0, 4, step, 0, unroll=4)
    for_queries.wait()


def keys_values(x, w):
    rows = x.shape[0]
    whole = pl.BlockSpec(memory_space=pltpu.VMEM)
    return pl.pallas_call(
        kv_kernel,
        in_specs=[whole, pl.BlockSpec(memory_space=pltpu.HBM)],
        out_specs=[whole, whole, whole],
        out_shape=[
            jax.ShapeDtypeStruct((rows, 2 * HW), BF),
            jax.ShapeDtypeStruct((rows, WIDTH), BF),
            jax.ShapeDtypeStruct((WIDTH, HW), BF),
        ],
        scratch_shapes=[pltpu.VMEM((WIDTH, 2 * HW), BF), pltpu.SemaphoreType.DMA((5,))],
        compiler_params=params(24),
        cost_estimate=HEAVY,
        name="keys_values",
    )(x, pltpu.with_memory_space_constraint(w, pltpu.HBM))


def q_kernel(norm_ref, w_ref, q_ref):
    def step(j, carry):
        y = jnp.dot(norm_ref[...], w_ref[:, block(j)], preferred_element_type=F32)
        q_ref[0, :, block(j)] = (y * QSCALE).astype(BF)
        return carry

    lax.fori_loop(0, 2, step, 0, unroll=2)


def queries(norm, w):
    whole = pl.BlockSpec(memory_space=pltpu.VMEM)
    return pl.pallas_call(
        q_kernel,
        in_specs=[whole, whole],
        out_specs=whole,
        out_shape=jax.ShapeDtypeStruct((1, norm.shape[0], HW), BF),
        compiler_params=params(16),
        cost_estimate=LIGHT,
        name="queries",
    )(norm, w)


def spatial_kernel(which, q_ref, *refs):
    count = len(which)
    kv_refs, o_refs = refs[: -count - 6], refs[-count - 6 : -6]
    keys, values, s_a, s_b, m_a, m_b = refs[-6:]
    pairs, rows = H // 2, o_refs[0].shape[0]
    width = keys.shape[0]
    groups = pairs // width
    low = lax.broadcasted_iota(jnp.int32, (rows, 128), 1) < HD
    zero = jnp.zeros((rows, 128), BF)
    for e in range(width):
        values[e, :, 128:] = jnp.ones((values.shape[1], 128), BF)

    def columns(pair):
        if isinstance(pair, int):
            return slice(pair * 128, pair * 128 + 128)
        return pl.ds(pl.multiple_of(pair * 128, 128), 128)

    def load(pair, held, e):
        lo = 0
        for ref in kv_refs:
            held[e, lo : lo + ref.shape[0], :128] = ref[:, columns(pair)]
            lo += ref.shape[0]

    def score(group, e, c, head, s_ref, m_ref):
        slot = (e * count + c) * 2 + head
        q = q_ref[which[c], :, columns(width * group + e)]
        q = jnp.where(low, q, zero) if head == 0 else jnp.where(low, zero, q)
        s = nt_dot(q, keys[e])
        s_ref[slot] = s
        m_ref[slot] = jnp.broadcast_to(jnp.max(s, axis=-1, keepdims=True), (rows, 128))

    def weigh(e, c, head, s_ref, m_ref):
        slot = (e * count + c) * 2 + head
        p = jnp.exp2(s_ref[slot] - m_ref[slot, :, :1]).astype(BF)
        o = jnp.dot(p, values[e], preferred_element_type=F32)
        return o[:, :128] / o[:, 128:]

    def phase(group, later, now, after):
        for e in range(width):
            load(width * group + e + pairs, values, e)
            if later is not None:
                load(width * later + e, keys, e)
        for e in range(width):
            for c in range(count):
                out = []
                for head in range(2):
                    if later is not None:
                        score(later, e, c, head, *after)
                    out.append(weigh(e, c, head, *now))
                o_refs[c][:, columns(width * group + e)] = jnp.where(low, out[0], out[1]).astype(BF)

    first, second = (s_a, m_a), (s_b, m_b)
    for e in range(width):
        load(e, keys, e)
        for c in range(count):
            for head in range(2):
                score(0, e, c, head, *first)

    def step(i, carry):
        phase(2 * i, 2 * i + 1, first, second)
        phase(2 * i + 1, 2 * i + 2, second, first)
        return carry

    lax.fori_loop(0, groups // 2 - 1, step, 0)
    phase(groups - 2, groups - 1, first, second)
    phase(groups - 1, None, second, first)


def spatial_attention(q, kvs, which):
    rows, total, count = q.shape[1], sum(kv.shape[0] for kv in kvs), len(which)
    width = 4 // count
    heads = 2 * width * count
    whole = pl.BlockSpec(memory_space=pltpu.VMEM)
    return pl.pallas_call(
        functools.partial(spatial_kernel, which),
        in_specs=[whole] * (1 + len(kvs)),
        out_specs=[whole] * count,
        out_shape=[jax.ShapeDtypeStruct((rows, HW), BF)] * count,
        scratch_shapes=[pltpu.VMEM((width, total, 128), BF), pltpu.VMEM((width, total, 256), BF)]
        + [pltpu.VMEM((heads, rows, total), F32)] * 2
        + [pltpu.VMEM((heads, rows, 128), F32)] * 2,
        compiler_params=params(24),
        cost_estimate=pl.CostEstimate(
            flops=count * rows * total * HW,
            bytes_accessed=1_000_000,
            transcendentals=0,
        ),
        name="spatial_attention",
    )(q, *kvs)


def reorder(to_patch_major):
    row = lax.broadcasted_iota(jnp.int32, (64, 64), 0)
    col = lax.broadcasted_iota(jnp.int32, (64, 64), 1)
    if to_patch_major:
        return (col == (row % 4) * 16 + row // 4).astype(BF)
    return (col == (row % 16) * 4 + row // 16).astype(BF)


def home(scalars, d):
    return lax.rem(scalars[2] + 4 - d, 4)


def middle_of(scalars, f, s_ref, x_ref, w_ref):
    valid = (scalars[0] + f < scalars[1]).astype(F32)
    branch = jnp.dot(s_ref[...], w_ref[...], preferred_element_type=F32)
    return (x_ref[f].astype(F32) + valid * branch).astype(BF)


def early_kernel(distances, scalars, *refs):
    s_refs, (x_ref, w_ref, middle_ref, norm_ref) = refs[:-4], refs[-4:]
    for d, s_ref in zip(distances, s_refs):
        f = home(scalars, d)
        middle = middle_of(scalars, f, s_ref, x_ref, w_ref)
        middle_ref[f] = middle
        norm_ref[f] = normalise(middle.astype(F32))


def early_rows(scalars, blocks, distances, video, w):
    whole = pl.BlockSpec(memory_space=pltpu.VMEM)
    return pl.pallas_call(
        functools.partial(early_kernel, distances),
        in_specs=[pl.BlockSpec(memory_space=pltpu.SMEM)] + [whole] * (2 + len(blocks)),
        out_specs=[whole, whole],
        out_shape=[jax.ShapeDtypeStruct((4, 144, WIDTH), BF)] * 2,
        compiler_params=params(16),
        cost_estimate=pl.CostEstimate(
            flops=2 * len(blocks) * 144 * HW * WIDTH, bytes_accessed=8_000_000, transcendentals=0
        ),
        name="early_rows",
    )(scalars, *blocks, video, w)


def late_kernel(distance, scalars, s_ref, norm_ref, x_ref, w_ref, middle_ref, send_ref, late):
    last = home(scalars, distance)
    middle = middle_of(scalars, last, s_ref, x_ref, w_ref)
    middle_ref[...] = middle
    late[...] = normalise(middle.astype(F32))
    move = reorder(True)
    for b in range(9):
        rows = slice(b * 16, b * 16 + 16)
        parts = [jnp.where(last == f, late[rows, :], norm_ref[f, rows, :]) for f in range(4)]
        moved = jnp.dot(move, jnp.concatenate(parts, axis=0), preferred_element_type=F32)
        send_ref[rows] = moved.astype(BF).reshape(16, 4, WIDTH)


def late_rows(scalars, spatial, norm, distance, video, w):
    whole = pl.BlockSpec(memory_space=pltpu.VMEM)
    return pl.pallas_call(
        functools.partial(late_kernel, distance),
        in_specs=[pl.BlockSpec(memory_space=pltpu.SMEM)] + [whole] * 4,
        out_specs=[whole, whole],
        out_shape=[
            jax.ShapeDtypeStruct((144, WIDTH), BF),
            jax.ShapeDtypeStruct((144, 4, WIDTH), BF),
        ],
        scratch_shapes=[pltpu.VMEM((144, WIDTH), BF)],
        compiler_params=params(16),
        cost_estimate=pl.CostEstimate(
            flops=2 * 144 * HW * WIDTH, bytes_accessed=8_000_000, transcendentals=0
        ),
        name="late_rows",
    )(scalars, spatial, norm, video, w)


def temporal_kernel(n, scalars, x_ref, w_ref, o_ref, rows_ref):
    for i in range(n):
        rows_ref[64 * i : 64 * i + 64, :] = x_ref[:, i].reshape(64, WIDTH)
    limit = scalars[1]
    head_row = lax.broadcasted_iota(jnp.int32, (256, 256), 0) // HD
    head_col = lax.broadcasted_iota(jnp.int32, (256, 256), 1) // HD
    same = head_row == head_col
    zero = jnp.zeros((256, 256), BF)
    key_valid = lax.broadcasted_iota(jnp.int32, (4, 64, 64), 1) < limit

    def step(g, carry):
        def project(part):
            cols = pl.ds(pl.multiple_of(part * HW + g * 256, 128), 256)
            return jnp.dot(rows_ref[...], w_ref[:, cols], preferred_element_type=F32)

        q = (project(0) * QSCALE).astype(BF)
        k = project(1).astype(BF)
        v = project(2).astype(BF)
        scores, weights = [], []
        for i in range(n):
            rows = slice(64 * i, 64 * i + 64)
            k4 = jnp.where(same, jnp.concatenate([k[rows]] * 4, axis=0), zero)
            scores.append(nt_dot(k4, q[rows]).reshape(4, 64, 64))
        for i in range(n):
            s = jnp.where(key_valid, scores[i], -1e30)
            p = jnp.exp2(s - jnp.max(s, axis=1, keepdims=True))
            p = p / jnp.sum(p, axis=1, keepdims=True)
            weights.append(p.reshape(256, 64).astype(BF))
        cols = pl.ds(pl.multiple_of(g * 256, 128), 256)
        for i in range(n):
            rows = slice(64 * i, 64 * i + 64)
            v4 = jnp.where(same, jnp.concatenate([v[rows]] * 4, axis=0), zero)
            o_ref[:, i, :, cols] = tn_dot(weights[i], v4).astype(BF).reshape(16, 4, 256)
        return carry

    lax.fori_loop(0, 4, step, 0, unroll=4)


def temporal_attention(scalars, x, w, n):
    rows = 64 * n
    whole = pl.BlockSpec(memory_space=pltpu.VMEM)
    return pl.pallas_call(
        functools.partial(temporal_kernel, n),
        in_specs=[pl.BlockSpec(memory_space=pltpu.SMEM), whole, whole],
        out_specs=whole,
        out_shape=jax.ShapeDtypeStruct((TM, n, 4, HW), BF),
        scratch_shapes=[pltpu.VMEM((rows, WIDTH), BF)],
        compiler_params=params(24),
        cost_estimate=pl.CostEstimate(
            flops=2 * rows * WIDTH * 3 * HW, bytes_accessed=14_000_000, transcendentals=0
        ),
        name="temporal_attention",
    )(scalars, x, w)


def encoded_kernel(distance, scalars, t_ref, m_ref, late_ref, w_ref, o_ref, rows_ref, held, sem):
    last = home(scalars, distance)
    move = reorder(False)
    for b in range(9):
        block = t_ref[b * 16 : b * 16 + 16].reshape(64, HW)
        moved = jnp.dot(move, block, preferred_element_type=F32).astype(BF)
        for f in range(4):
            lo = f * 144 + b * 16
            rows_ref[lo : lo + 16, :] = moved[f * 16 : f * 16 + 16]
    first, limit = scalars[0], scalars[1]

    def leave(j):
        cols = pl.ds(pl.multiple_of(j * 512, 128), 512)
        return pltpu.make_async_copy(held.at[:, :, cols], o_ref.at[:, :, cols], sem.at[j])

    def project(j, carry):
        cols = pl.ds(pl.multiple_of(j * 512, 128), 512)
        branch = jnp.dot(rows_ref[...], w_ref[:, cols], preferred_element_type=F32)
        for f in range(4):
            valid = (first + f < limit).astype(F32)
            own = branch[f * 144 : (f + 1) * 144]
            middle = jnp.where(last == f, late_ref[:, cols], m_ref[f, :, cols])
            held[f, :, cols] = (middle.astype(F32) + valid * own).astype(BF)
        leave(j).start()
        return carry

    lax.fori_loop(0, 3, project, 0, unroll=3)
    for j in range(3):
        leave(j).wait()


def encoded_rows(scalars, temporal, middle, late, distance, w):
    whole = pl.BlockSpec(memory_space=pltpu.VMEM)
    return pl.pallas_call(
        functools.partial(encoded_kernel, distance),
        in_specs=[pl.BlockSpec(memory_space=pltpu.SMEM)] + [whole] * 4,
        out_specs=pl.BlockSpec(memory_space=pltpu.HBM),
        out_shape=jax.ShapeDtypeStruct((4, 144, WIDTH), BF),
        scratch_shapes=[
            pltpu.VMEM((4 * 144, HW), BF),
            pltpu.VMEM((4, 144, WIDTH), BF),
            pltpu.SemaphoreType.DMA((3,)),
        ],
        compiler_params=params(24),
        cost_estimate=pl.CostEstimate(
            flops=8 * 144 * HW * WIDTH, bytes_accessed=8_000_000, transcendentals=0
        ),
        name="encoded_rows",
    )(scalars, temporal, middle, late, w)


def along_z(x, distance):
    pairs = [(i, (i + 2 * distance) % 8) for i in range(8)]
    return lax.ppermute(x, "space", pairs)


def over_tm(x):
    return lax.all_to_all(x, "tm", split_axis=0, concat_axis=0, tiled=True)


def per_device(video, frame_count, qkv_space, out_space, qkv_time, out_time):
    first = lax.axis_index("tm") * video.shape[0]
    z = lax.axis_index("space") // 2
    scalars = jnp.stack([first, frame_count[0], z]).astype(jnp.int32)

    def from_chip(e, sent):
        return along_z(sent, 4 - e)

    sent = {
        e: lax.dynamic_index_in_dim(video, lax.rem(z + 4 - e, 4), 0, keepdims=False) for e in (1, 3, 2)
    }
    near = [from_chip(e, sent[e]) for e in (1, 3)]
    kv_own, q_own = own_block(scalars, video, qkv_space)
    kv_own_other = lax.ppermute(kv_own, "space", SWAP)
    late, kv_own, *near = lax.optimization_barrier((sent[2], kv_own, *near))
    far = from_chip(2, late)
    kv_near, q_near = near_blocks(near, qkv_space)
    kv_near_other = lax.ppermute(kv_near, "space", SWAP)
    far, kv_near = lax.optimization_barrier((far, kv_near))
    kv_far, norm1, w_q = keys_values(far, qkv_space)
    kv_far_other = lax.ppermute(kv_far, "space", SWAP)
    q_far = queries(norm1, w_q)
    kvs = (kv_near, kv_far, kv_own, kv_near_other, kv_far_other, kv_own_other)
    back = {}
    for blocks in ((1, 3), (2,)):
        results = spatial_attention(q_near if 1 in blocks else q_far, kvs, range(len(blocks)))
        q_far, q_own, *results = lax.optimization_barrier((q_far, q_own, *results))
        for e, o in zip(blocks, results):
            back[e] = along_z(o, e)
    (back[0],) = spatial_attention(q_own, kvs, range(1))
    early = tuple(d for d in (0, 1, 2, 3) if d != LATE)
    middle, norm2 = early_rows(scalars, [back[d] for d in early], early, video, out_space)
    late, send = late_rows(scalars, back[LATE], norm2, LATE, video, out_space)
    rows = over_tm(send.reshape(TM, 9, 4, WIDTH))
    temporal = temporal_attention(scalars, rows, qkv_time, 9)
    temporal = over_tm(temporal).reshape(144, 4, HW)
    return encoded_rows(scalars, temporal, middle, late, LATE, out_time)


def solution(mesh):
    return jax.shard_map(
        per_device,
        mesh=mesh,
        in_specs=(P("tm", "space", None), P(), P(), P(), P(), P()),
        out_specs=P("tm", "space", None),
        check_vma=False,
    )
```

```python
import functools

import jax
import jax.numpy as jnp
from jax import lax
from jax.experimental import pallas as pl
from jax.experimental.pallas import tpu as pltpu
from jax.sharding import PartitionSpec as P

H = 16
HD = 64
WIDTH = 1536
HW = H * HD
TM = 16
QSCALE = 0.125 * 1.4426950408889634
LATE = 2
SWAP = [(i, i ^ 1) for i in range(8)]
BF = jnp.bfloat16
F32 = jnp.float32


HEAVY = pl.CostEstimate(flops=20_000_000_000, bytes_accessed=1_000_000, transcendentals=0)
LIGHT = pl.CostEstimate(flops=100_000_000, bytes_accessed=1_000_000, transcendentals=0)


def params(mebibytes):
    return pltpu.CompilerParams(vmem_limit_bytes=mebibytes * 1024 * 1024)


def normalise(wide):
    center = wide - jnp.mean(wide, axis=-1, keepdims=True)
    spread = jnp.mean(center * center, axis=-1, keepdims=True)
    return (center * lax.rsqrt(spread + 1e-06)).astype(BF)


def nt_dot(a, b):
    return lax.dot_general(a, b, (((1,), (1,)), ((), ())), preferred_element_type=F32)


def tn_dot(a, b):
    return lax.dot_general(a, b, (((0,), (0,)), ((), ())), preferred_element_type=F32)


def block(j):
    return pl.ds(pl.multiple_of(j * 512, 128), 512)


def own_kernel(scalars, video_ref, w_ref, kv_ref, q_ref, x_ref, norm_ref, held, sem):
    mine = pltpu.make_async_copy(video_ref.at[scalars[2]], x_ref, sem.at[6])
    mine.start()

    def fetch(j):
        return pltpu.make_async_copy(w_ref.at[:, block(j)], held.at[:, block(j)], sem.at[j])

    for j in (2, 3, 4, 5, 0, 1):
        fetch(j).start()
    mine.wait()

    def norm(i, carry):
        rows = pl.ds(pl.multiple_of(i * 48, 48), 48)
        norm_ref[rows, :] = normalise(x_ref[rows, :].astype(F32))
        return carry

    lax.fori_loop(0, 3, norm, 0)

    def key_value(j, carry):
        fetch(j).wait()
        y = jnp.dot(norm_ref[...], held[:, block(j)], preferred_element_type=F32)
        kv_ref[:, block(j - 2)] = y.astype(BF)
        return carry

    def query(j, carry):
        fetch(j).wait()
        y = jnp.dot(norm_ref[...], held[:, block(j)], preferred_element_type=F32)
        q_ref[0, :, block(j)] = (y * QSCALE).astype(BF)
        return carry

    lax.fori_loop(2, 6, key_value, 0)
    lax.fori_loop(0, 2, query, 0)


def own_block(scalars, video, w):
    rows = video.shape[1]
    whole = pl.BlockSpec(memory_space=pltpu.VMEM)
    far = pl.BlockSpec(memory_space=pltpu.HBM)
    return pl.pallas_call(
        own_kernel,
        in_specs=[pl.BlockSpec(memory_space=pltpu.SMEM), far, far],
        out_specs=[whole, whole],
        out_shape=[
            jax.ShapeDtypeStruct((rows, 2 * HW), BF),
            jax.ShapeDtypeStruct((1, rows, HW), BF),
        ],
        scratch_shapes=[
            pltpu.VMEM((rows, WIDTH), BF),
            pltpu.VMEM((rows, WIDTH), BF),
            pltpu.VMEM((WIDTH, 3 * HW), BF),
            pltpu.SemaphoreType.DMA((7,)),
        ],
        compiler_params=params(24),
        cost_estimate=LIGHT,
        name="own_block",
    )(
        scalars,
        pltpu.with_memory_space_constraint(video, pltpu.HBM),
        pltpu.with_memory_space_constraint(w, pltpu.HBM),
    )


def near_kernel(count, *refs):
    x_refs, (w_ref, kv_ref, q_ref, held, norm_ref, sem) = refs[:count], refs[count:]

    def fetch(j):
        return pltpu.make_async_copy(w_ref.at[:, block(j)], held.at[:, block(j)], sem.at[j])

    for j in (2, 3, 4, 5, 0, 1):
        fetch(j).start()
    normalise_blocks(x_refs, norm_ref)

    def key_value(j, carry):
        fetch(j).wait()
        y = jnp.dot(norm_ref[...], held[:, block(j)], preferred_element_type=F32)
        kv_ref[:, block(j - 2)] = y.astype(BF)
        return carry

    def query(j, carry):
        fetch(j).wait()
        y = jnp.dot(norm_ref[...], held[:, block(j)], preferred_element_type=F32)
        q = (y * QSCALE).astype(BF)
        for b in range(count):
            q_ref[b, :, block(j)] = q[b * 144 : (b + 1) * 144]
        return carry

    lax.fori_loop(2, 6, key_value, 0)
    lax.fori_loop(0, 2, query, 0)


def normalise_blocks(x_refs, norm_ref):
    for b, x_ref in enumerate(x_refs):

        def norm(i, carry):
            lo = pl.multiple_of(i * 48, 48)
            norm_ref[pl.ds(b * 144 + lo, 48), :] = normalise(x_ref[pl.ds(lo, 48), :].astype(F32))
            return carry

        lax.fori_loop(0, 3, norm, 0, unroll=True)


def near_blocks(blocks, w):
    count, rows = len(blocks), 144 * len(blocks)
    whole = pl.BlockSpec(memory_space=pltpu.VMEM)
    return pl.pallas_call(
        functools.partial(near_kernel, count),
        in_specs=[whole] * count + [pl.BlockSpec(memory_space=pltpu.HBM)],
        out_specs=[whole, whole, whole],
        out_shape=[
            jax.ShapeDtypeStruct((rows, 2 * HW), BF),
            jax.ShapeDtypeStruct((count, 144, HW), BF),
            jax.ShapeDtypeStruct((WIDTH, 3 * HW), BF),
        ],
        scratch_shapes=[
            pltpu.VMEM((rows, WIDTH), BF),
            pltpu.SemaphoreType.DMA((6,)),
        ],
        compiler_params=params(24),
        cost_estimate=LIGHT,
        name="near_blocks",
    )(*blocks, pltpu.with_memory_space_constraint(w, pltpu.HBM))


def kv_kernel(x_ref, w_ref, kv_ref, norm_ref):
    normalise_blocks([x_ref], norm_ref)

    def step(j, carry):
        y = jnp.dot(norm_ref[...], w_ref[:, block(j + 2)], preferred_element_type=F32)
        kv_ref[:, block(j)] = y.astype(BF)
        return carry

    lax.fori_loop(0, 4, step, 0, unroll=4)


def keys_values(x, w):
    rows = x.shape[0]
    whole = pl.BlockSpec(memory_space=pltpu.VMEM)
    return pl.pallas_call(
        kv_kernel,
        in_specs=[whole, whole],
        out_specs=[whole, whole],
        out_shape=[
            jax.ShapeDtypeStruct((rows, 2 * HW), BF),
            jax.ShapeDtypeStruct((rows, WIDTH), BF),
        ],
        compiler_params=params(16),
        cost_estimate=HEAVY,
        name="keys_values",
    )(x, w)


def q_kernel(norm_ref, w_ref, q_ref):
    def step(j, carry):
        y = jnp.dot(norm_ref[...], w_ref[:, block(j)], preferred_element_type=F32)
        q_ref[0, :, block(j)] = (y * QSCALE).astype(BF)
        return carry

    lax.fori_loop(0, 2, step, 0, unroll=2)


def queries(norm, w):
    whole = pl.BlockSpec(memory_space=pltpu.VMEM)
    return pl.pallas_call(
        q_kernel,
        in_specs=[whole, whole],
        out_specs=whole,
        out_shape=jax.ShapeDtypeStruct((1, norm.shape[0], HW), BF),
        compiler_params=params(16),
        cost_estimate=LIGHT,
        name="queries",
    )(norm, w)


def spatial_kernel(which, q_ref, *refs):
    count = len(which)
    kv_refs, o_refs = refs[: -count - 6], refs[-count - 6 : -6]
    keys, values, s_a, s_b, m_a, m_b = refs[-6:]
    pairs, rows = H // 2, o_refs[0].shape[0]
    width = keys.shape[0]
    groups = pairs // width
    low = lax.broadcasted_iota(jnp.int32, (rows, 128), 1) < HD
    zero = jnp.zeros((rows, 128), BF)
    for e in range(width):
        values[e, :, 128:] = jnp.ones((values.shape[1], 128), BF)

    def columns(pair):
        if isinstance(pair, int):
            return slice(pair * 128, pair * 128 + 128)
        return pl.ds(pl.multiple_of(pair * 128, 128), 128)

    def load(pair, held, e):
        lo = 0
        for ref in kv_refs:
            held[e, lo : lo + ref.shape[0], :128] = ref[:, columns(pair)]
            lo += ref.shape[0]

    def score(group, e, c, head, s_ref, m_ref):
        slot = (e * count + c) * 2 + head
        q = q_ref[which[c], :, columns(width * group + e)]
        q = jnp.where(low, q, zero) if head == 0 else jnp.where(low, zero, q)
        s = nt_dot(q, keys[e])
        s_ref[slot] = s
        m_ref[slot] = jnp.broadcast_to(jnp.max(s, axis=-1, keepdims=True), (rows, 128))

    def weigh(e, c, head, s_ref, m_ref):
        slot = (e * count + c) * 2 + head
        p = jnp.exp2(s_ref[slot] - m_ref[slot, :, :1]).astype(BF)
        o = jnp.dot(p, values[e], preferred_element_type=F32)
        return o[:, :128] / o[:, 128:]

    def phase(group, later, now, after):
        for e in range(width):
            load(width * group + e + pairs, values, e)
            if later is not None:
                load(width * later + e, keys, e)
        for e in range(width):
            for c in range(count):
                out = []
                for head in range(2):
                    if later is not None:
                        score(later, e, c, head, *after)
                    out.append(weigh(e, c, head, *now))
                o_refs[c][:, columns(width * group + e)] = jnp.where(low, out[0], out[1]).astype(BF)

    first, second = (s_a, m_a), (s_b, m_b)
    for e in range(width):
        load(e, keys, e)
        for c in range(count):
            for head in range(2):
                score(0, e, c, head, *first)

    def step(i, carry):
        phase(2 * i, 2 * i + 1, first, second)
        phase(2 * i + 1, 2 * i + 2, second, first)
        return carry

    lax.fori_loop(0, groups // 2 - 1, step, 0)
    phase(groups - 2, groups - 1, first, second)
    phase(groups - 1, None, second, first)


def spatial_attention(q, kvs, which):
    rows, total, count = q.shape[1], sum(kv.shape[0] for kv in kvs), len(which)
    width = 4 // count
    heads = 2 * width * count
    whole = pl.BlockSpec(memory_space=pltpu.VMEM)
    return pl.pallas_call(
        functools.partial(spatial_kernel, which),
        in_specs=[whole] * (1 + len(kvs)),
        out_specs=[whole] * count,
        out_shape=[jax.ShapeDtypeStruct((rows, HW), BF)] * count,
        scratch_shapes=[pltpu.VMEM((width, total, 128), BF), pltpu.VMEM((width, total, 256), BF)]
        + [pltpu.VMEM((heads, rows, total), F32)] * 2
        + [pltpu.VMEM((heads, rows, 128), F32)] * 2,
        compiler_params=params(24),
        cost_estimate=pl.CostEstimate(
            flops=count * rows * total * HW,
            bytes_accessed=1_000_000,
            transcendentals=0,
        ),
        name="spatial_attention",
    )(q, *kvs)


def reorder(to_patch_major):
    row = lax.broadcasted_iota(jnp.int32, (64, 64), 0)
    col = lax.broadcasted_iota(jnp.int32, (64, 64), 1)
    if to_patch_major:
        return (col == (row % 4) * 16 + row // 4).astype(BF)
    return (col == (row % 16) * 4 + row // 16).astype(BF)


def home(scalars, d):
    return lax.rem(scalars[2] + 4 - d, 4)


def middle_of(scalars, f, s_ref, x_ref, w_ref):
    valid = (scalars[0] + f < scalars[1]).astype(F32)
    branch = jnp.dot(s_ref[...], w_ref[...], preferred_element_type=F32)
    return (x_ref[f].astype(F32) + valid * branch).astype(BF)


def early_kernel(distances, scalars, *refs):
    s_refs, (x_ref, w_ref, middle_ref, norm_ref) = refs[:-4], refs[-4:]
    for d, s_ref in zip(distances, s_refs):
        f = home(scalars, d)
        middle = middle_of(scalars, f, s_ref, x_ref, w_ref)
        middle_ref[f] = middle
        norm_ref[f] = normalise(middle.astype(F32))


def early_rows(scalars, blocks, distances, video, w):
    whole = pl.BlockSpec(memory_space=pltpu.VMEM)
    return pl.pallas_call(
        functools.partial(early_kernel, distances),
        in_specs=[pl.BlockSpec(memory_space=pltpu.SMEM)] + [whole] * (2 + len(blocks)),
        out_specs=[whole, whole],
        out_shape=[jax.ShapeDtypeStruct((4, 144, WIDTH), BF)] * 2,
        compiler_params=params(16),
        cost_estimate=pl.CostEstimate(
            flops=2 * len(blocks) * 144 * HW * WIDTH, bytes_accessed=8_000_000, transcendentals=0
        ),
        name="early_rows",
    )(scalars, *blocks, video, w)


def late_kernel(distance, scalars, s_ref, norm_ref, x_ref, w_ref, middle_ref, send_ref, late):
    last = home(scalars, distance)
    middle = middle_of(scalars, last, s_ref, x_ref, w_ref)
    middle_ref[...] = middle
    late[...] = normalise(middle.astype(F32))
    move = reorder(True)
    for b in range(9):
        rows = slice(b * 16, b * 16 + 16)
        parts = [jnp.where(last == f, late[rows, :], norm_ref[f, rows, :]) for f in range(4)]
        moved = jnp.dot(move, jnp.concatenate(parts, axis=0), preferred_element_type=F32)
        send_ref[rows] = moved.astype(BF).reshape(16, 4, WIDTH)


def late_rows(scalars, spatial, norm, distance, video, w):
    whole = pl.BlockSpec(memory_space=pltpu.VMEM)
    return pl.pallas_call(
        functools.partial(late_kernel, distance),
        in_specs=[pl.BlockSpec(memory_space=pltpu.SMEM)] + [whole] * 4,
        out_specs=[whole, whole],
        out_shape=[
            jax.ShapeDtypeStruct((144, WIDTH), BF),
            jax.ShapeDtypeStruct((144, 4, WIDTH), BF),
        ],
        scratch_shapes=[pltpu.VMEM((144, WIDTH), BF)],
        compiler_params=params(16),
        cost_estimate=pl.CostEstimate(
            flops=2 * 144 * HW * WIDTH, bytes_accessed=8_000_000, transcendentals=0
        ),
        name="late_rows",
    )(scalars, spatial, norm, video, w)


def temporal_kernel(n, scalars, x_ref, w_ref, o_ref, rows_ref):
    for i in range(n):
        rows_ref[64 * i : 64 * i + 64, :] = x_ref[:, i].reshape(64, WIDTH)
    limit = scalars[1]
    head_row = lax.broadcasted_iota(jnp.int32, (256, 256), 0) // HD
    head_col = lax.broadcasted_iota(jnp.int32, (256, 256), 1) // HD
    same = head_row == head_col
    zero = jnp.zeros((256, 256), BF)
    key_valid = lax.broadcasted_iota(jnp.int32, (4, 64, 64), 1) < limit

    def step(g, carry):
        def project(part):
            cols = pl.ds(pl.multiple_of(part * HW + g * 256, 128), 256)
            return jnp.dot(rows_ref[...], w_ref[:, cols], preferred_element_type=F32)

        q = (project(0) * QSCALE).astype(BF)
        k = project(1).astype(BF)
        v = project(2).astype(BF)
        scores, weights = [], []
        for i in range(n):
            rows = slice(64 * i, 64 * i + 64)
            k4 = jnp.where(same, jnp.concatenate([k[rows]] * 4, axis=0), zero)
            scores.append(nt_dot(k4, q[rows]).reshape(4, 64, 64))
        for i in range(n):
            s = jnp.where(key_valid, scores[i], -1e30)
            p = jnp.exp2(s - jnp.max(s, axis=1, keepdims=True))
            p = p / jnp.sum(p, axis=1, keepdims=True)
            weights.append(p.reshape(256, 64).astype(BF))
        cols = pl.ds(pl.multiple_of(g * 256, 128), 256)
        for i in range(n):
            rows = slice(64 * i, 64 * i + 64)
            v4 = jnp.where(same, jnp.concatenate([v[rows]] * 4, axis=0), zero)
            o_ref[:, i, :, cols] = tn_dot(weights[i], v4).astype(BF).reshape(16, 4, 256)
        return carry

    lax.fori_loop(0, 4, step, 0, unroll=4)


def temporal_attention(scalars, x, w, n):
    rows = 64 * n
    whole = pl.BlockSpec(memory_space=pltpu.VMEM)
    return pl.pallas_call(
        functools.partial(temporal_kernel, n),
        in_specs=[pl.BlockSpec(memory_space=pltpu.SMEM), whole, whole],
        out_specs=whole,
        out_shape=jax.ShapeDtypeStruct((TM, n, 4, HW), BF),
        scratch_shapes=[pltpu.VMEM((rows, WIDTH), BF)],
        compiler_params=params(24),
        cost_estimate=pl.CostEstimate(
            flops=2 * rows * WIDTH * 3 * HW, bytes_accessed=14_000_000, transcendentals=0
        ),
        name="temporal_attention",
    )(scalars, x, w)


def encoded_kernel(distance, scalars, t_ref, m_ref, late_ref, w_ref, o_ref, rows_ref, held, sem):
    last = home(scalars, distance)
    move = reorder(False)
    for b in range(9):
        block = t_ref[b * 16 : b * 16 + 16].reshape(64, HW)
        moved = jnp.dot(move, block, preferred_element_type=F32).astype(BF)
        for f in range(4):
            lo = f * 144 + b * 16
            rows_ref[lo : lo + 16, :] = moved[f * 16 : f * 16 + 16]
    first, limit = scalars[0], scalars[1]

    def leave(j):
        cols = pl.ds(pl.multiple_of(j * 512, 128), 512)
        return pltpu.make_async_copy(held.at[:, :, cols], o_ref.at[:, :, cols], sem.at[j])

    def project(j, carry):
        cols = pl.ds(pl.multiple_of(j * 512, 128), 512)
        branch = jnp.dot(rows_ref[...], w_ref[:, cols], preferred_element_type=F32)
        for f in range(4):
            valid = (first + f < limit).astype(F32)
            own = branch[f * 144 : (f + 1) * 144]
            middle = jnp.where(last == f, late_ref[:, cols], m_ref[f, :, cols])
            held[f, :, cols] = (middle.astype(F32) + valid * own).astype(BF)
        leave(j).start()
        return carry

    lax.fori_loop(0, 3, project, 0, unroll=3)
    for j in range(3):
        leave(j).wait()


def encoded_rows(scalars, temporal, middle, late, distance, w):
    whole = pl.BlockSpec(memory_space=pltpu.VMEM)
    return pl.pallas_call(
        functools.partial(encoded_kernel, distance),
        in_specs=[pl.BlockSpec(memory_space=pltpu.SMEM)] + [whole] * 4,
        out_specs=pl.BlockSpec(memory_space=pltpu.HBM),
        out_shape=jax.ShapeDtypeStruct((4, 144, WIDTH), BF),
        scratch_shapes=[
            pltpu.VMEM((4 * 144, HW), BF),
            pltpu.VMEM((4, 144, WIDTH), BF),
            pltpu.SemaphoreType.DMA((3,)),
        ],
        compiler_params=params(24),
        cost_estimate=pl.CostEstimate(
            flops=8 * 144 * HW * WIDTH, bytes_accessed=8_000_000, transcendentals=0
        ),
        name="encoded_rows",
    )(scalars, temporal, middle, late, w)


def along_z(x, distance):
    pairs = [(i, (i + 2 * distance) % 8) for i in range(8)]
    return lax.ppermute(x, "space", pairs)


def over_tm(x):
    return lax.all_to_all(x, "tm", split_axis=0, concat_axis=0, tiled=True)


def per_device(video, frame_count, qkv_space, out_space, qkv_time, out_time):
    first = lax.axis_index("tm") * video.shape[0]
    z = lax.axis_index("space") // 2
    scalars = jnp.stack([first, frame_count[0], z]).astype(jnp.int32)

    def from_chip(e, sent):
        return along_z(sent, 4 - e)

    sent = {
        e: lax.dynamic_index_in_dim(video, lax.rem(z + 4 - e, 4), 0, keepdims=False) for e in (1, 3, 2)
    }
    near = [from_chip(e, sent[e]) for e in (1, 3)]
    kv_own, q_own = own_block(scalars, video, qkv_space)
    kv_own_other = lax.ppermute(kv_own, "space", SWAP)
    late, kv_own, *near = lax.optimization_barrier((sent[2], kv_own, *near))
    far = from_chip(2, late)
    kv_near, q_near, w_held = near_blocks(near, qkv_space)
    kv_near_other = lax.ppermute(kv_near, "space", SWAP)
    far, kv_near = lax.optimization_barrier((far, kv_near))
    kv_far, norm1 = keys_values(far, w_held)
    kv_far_other = lax.ppermute(kv_far, "space", SWAP)
    q_far = queries(norm1, w_held)
    kvs = (kv_near, kv_far, kv_own, kv_near_other, kv_far_other, kv_own_other)
    back = {}
    for blocks in ((1, 3), (2,)):
        results = spatial_attention(q_near if 1 in blocks else q_far, kvs, range(len(blocks)))
        q_far, q_own, *results = lax.optimization_barrier((q_far, q_own, *results))
        for e, o in zip(blocks, results):
            back[e] = along_z(o, e)
    (back[0],) = spatial_attention(q_own, kvs, range(1))
    early = tuple(d for d in (0, 1, 2, 3) if d != LATE)
    middle, norm2 = early_rows(scalars, [back[d] for d in early], early, video, out_space)
    late, send = late_rows(scalars, back[LATE], norm2, LATE, video, out_space)
    rows = over_tm(send.reshape(TM, 9, 4, WIDTH))
    temporal = temporal_attention(scalars, rows, qkv_time, 9)
    temporal = over_tm(temporal).reshape(144, 4, HW)
    return encoded_rows(scalars, temporal, middle, late, LATE, out_time)


def solution(mesh):
    return jax.shard_map(
        per_device,
        mesh=mesh,
        in_specs=(P("tm", "space", None), P(), P(), P(), P(), P()),
        out_specs=P("tm", "space", None),
        check_vma=False,
    )
```

```python
import functools

import jax
import jax.numpy as jnp
from jax import lax
from jax.experimental import pallas as pl
from jax.experimental.pallas import tpu as pltpu
from jax.sharding import PartitionSpec as P

H = 16
HD = 64
WIDTH = 1536
HW = H * HD
TM = 16
QSCALE = 0.125 * 1.4426950408889634
LATE = 2
SWAP = [(i, i ^ 1) for i in range(8)]
BF = jnp.bfloat16
F32 = jnp.float32


HEAVY = pl.CostEstimate(flops=20_000_000_000, bytes_accessed=1_000_000, transcendentals=0)
LIGHT = pl.CostEstimate(flops=100_000_000, bytes_accessed=1_000_000, transcendentals=0)


def params(mebibytes):
    return pltpu.CompilerParams(vmem_limit_bytes=mebibytes * 1024 * 1024)


def normalise(wide):
    center = wide - jnp.mean(wide, axis=-1, keepdims=True)
    spread = jnp.mean(center * center, axis=-1, keepdims=True)
    return (center * lax.rsqrt(spread + 1e-06)).astype(BF)


def nt_dot(a, b):
    return lax.dot_general(a, b, (((1,), (1,)), ((), ())), preferred_element_type=F32)


def tn_dot(a, b):
    return lax.dot_general(a, b, (((0,), (0,)), ((), ())), preferred_element_type=F32)


def block(j):
    return pl.ds(pl.multiple_of(j * 512, 128), 512)


def own_kernel(scalars, video_ref, w_ref, kv_ref, q_ref, x_ref, norm_ref, held, sem):
    mine = pltpu.make_async_copy(video_ref.at[scalars[2]], x_ref, sem.at[6])
    mine.start()

    def fetch(j):
        return pltpu.make_async_copy(w_ref.at[:, block(j)], held.at[:, block(j)], sem.at[j])

    for j in (2, 3, 4, 5, 0, 1):
        fetch(j).start()
    mine.wait()

    def norm(i, carry):
        rows = pl.ds(pl.multiple_of(i * 48, 48), 48)
        norm_ref[rows, :] = normalise(x_ref[rows, :].astype(F32))
        return carry

    lax.fori_loop(0, 3, norm, 0)

    def key_value(j, carry):
        fetch(j).wait()
        y = jnp.dot(norm_ref[...], held[:, block(j)], preferred_element_type=F32)
        kv_ref[:, block(j - 2)] = y.astype(BF)
        return carry

    def query(j, carry):
        fetch(j).wait()
        y = jnp.dot(norm_ref[...], held[:, block(j)], preferred_element_type=F32)
        q_ref[0, :, block(j)] = (y * QSCALE).astype(BF)
        return carry

    lax.fori_loop(2, 6, key_value, 0)
    lax.fori_loop(0, 2, query, 0)


def own_block(scalars, video, w):
    rows = video.shape[1]
    whole = pl.BlockSpec(memory_space=pltpu.VMEM)
    far = pl.BlockSpec(memory_space=pltpu.HBM)
    return pl.pallas_call(
        own_kernel,
        in_specs=[pl.BlockSpec(memory_space=pltpu.SMEM), far, far],
        out_specs=[whole, whole],
        out_shape=[
            jax.ShapeDtypeStruct((rows, 2 * HW), BF),
            jax.ShapeDtypeStruct((1, rows, HW), BF),
        ],
        scratch_shapes=[
            pltpu.VMEM((rows, WIDTH), BF),
            pltpu.VMEM((rows, WIDTH), BF),
            pltpu.VMEM((WIDTH, 3 * HW), BF),
            pltpu.SemaphoreType.DMA((7,)),
        ],
        compiler_params=params(24),
        cost_estimate=LIGHT,
        name="own_block",
    )(
        scalars,
        pltpu.with_memory_space_constraint(video, pltpu.HBM),
        pltpu.with_memory_space_constraint(w, pltpu.HBM),
    )


def near_kernel(count, *refs):
    x_refs, (w_ref, kv_ref, q_ref, held, norm_ref, sem) = refs[:count], refs[count:]

    def fetch(j):
        return pltpu.make_async_copy(w_ref.at[:, block(j)], held.at[:, block(j)], sem.at[j])

    for j in (2, 3, 4, 5, 0, 1):
        fetch(j).start()
    normalise_blocks(x_refs, norm_ref)

    def key_value(j, carry):
        fetch(j).wait()
        y = jnp.dot(norm_ref[...], held[:, block(j)], preferred_element_type=F32)
        kv_ref[:, block(j - 2)] = y.astype(BF)
        return carry

    def query(j, carry):
        fetch(j).wait()
        y = jnp.dot(norm_ref[...], held[:, block(j)], preferred_element_type=F32)
        q = (y * QSCALE).astype(BF)
        for b in range(count):
            q_ref[b, :, block(j)] = q[b * 144 : (b + 1) * 144]
        return carry

    lax.fori_loop(2, 6, key_value, 0)
    lax.fori_loop(0, 2, query, 0)


def normalise_blocks(x_refs, norm_ref):
    for b, x_ref in enumerate(x_refs):

        def norm(i, carry):
            lo = pl.multiple_of(i * 48, 48)
            norm_ref[pl.ds(b * 144 + lo, 48), :] = normalise(x_ref[pl.ds(lo, 48), :].astype(F32))
            return carry

        lax.fori_loop(0, 3, norm, 0, unroll=True)


def near_blocks(blocks, w):
    count, rows = len(blocks), 144 * len(blocks)
    whole = pl.BlockSpec(memory_space=pltpu.VMEM)
    return pl.pallas_call(
        functools.partial(near_kernel, count),
        in_specs=[whole] * count + [pl.BlockSpec(memory_space=pltpu.HBM)],
        out_specs=[whole, whole, whole],
        out_shape=[
            jax.ShapeDtypeStruct((rows, 2 * HW), BF),
            jax.ShapeDtypeStruct((count, 144, HW), BF),
            jax.ShapeDtypeStruct((WIDTH, 3 * HW), BF),
        ],
        scratch_shapes=[
            pltpu.VMEM((rows, WIDTH), BF),
            pltpu.SemaphoreType.DMA((6,)),
        ],
        compiler_params=params(24),
        cost_estimate=LIGHT,
        name="near_blocks",
    )(*blocks, pltpu.with_memory_space_constraint(w, pltpu.HBM))


def kv_kernel(x_ref, w_ref, kv_ref, norm_ref):
    normalise_blocks([x_ref], norm_ref)

    def step(j, carry):
        y = jnp.dot(norm_ref[...], w_ref[:, block(j + 2)], preferred_element_type=F32)
        kv_ref[:, block(j)] = y.astype(BF)
        return carry

    lax.fori_loop(0, 4, step, 0, unroll=4)


def keys_values(x, w):
    rows = x.shape[0]
    whole = pl.BlockSpec(memory_space=pltpu.VMEM)
    return pl.pallas_call(
        kv_kernel,
        in_specs=[whole, whole],
        out_specs=[whole, whole],
        out_shape=[
            jax.ShapeDtypeStruct((rows, 2 * HW), BF),
            jax.ShapeDtypeStruct((rows, WIDTH), BF),
        ],
        compiler_params=params(16),
        cost_estimate=HEAVY,
        name="keys_values",
    )(x, w)


def q_kernel(norm_ref, w_ref, q_ref):
    def step(j, carry):
        y = jnp.dot(norm_ref[...], w_ref[:, block(j)], preferred_element_type=F32)
        q_ref[0, :, block(j)] = (y * QSCALE).astype(BF)
        return carry

    lax.fori_loop(0, 2, step, 0, unroll=2)


def queries(norm, w):
    whole = pl.BlockSpec(memory_space=pltpu.VMEM)
    return pl.pallas_call(
        q_kernel,
        in_specs=[whole, whole],
        out_specs=whole,
        out_shape=jax.ShapeDtypeStruct((1, norm.shape[0], HW), BF),
        compiler_params=params(16),
        cost_estimate=LIGHT,
        name="queries",
    )(norm, w)


def spatial_kernel(which, q_ref, *refs):
    count = len(which)
    kv_refs, o_refs = refs[: -count - 6], refs[-count - 6 : -6]
    keys, values, s_a, s_b, m_a, m_b = refs[-6:]
    pairs, rows = H // 2, o_refs[0].shape[0]
    width = keys.shape[0]
    groups = pairs // width
    low = lax.broadcasted_iota(jnp.int32, (rows, 128), 1) < HD
    zero = jnp.zeros((rows, 128), BF)
    for e in range(width):
        values[e, :, 128:] = jnp.ones((values.shape[1], 128), BF)

    def columns(pair):
        if isinstance(pair, int):
            return slice(pair * 128, pair * 128 + 128)
        return pl.ds(pl.multiple_of(pair * 128, 128), 128)

    def load(pair, held, e):
        lo = 0
        for ref in kv_refs:
            held[e, lo : lo + ref.shape[0], :128] = ref[:, columns(pair)]
            lo += ref.shape[0]

    def score(group, e, c, head, s_ref, m_ref):
        slot = (e * count + c) * 2 + head
        q = q_ref[which[c], :, columns(width * group + e)]
        q = jnp.where(low, q, zero) if head == 0 else jnp.where(low, zero, q)
        s = nt_dot(q, keys[e])
        s_ref[slot] = s
        m_ref[slot] = jnp.broadcast_to(jnp.max(s, axis=-1, keepdims=True), (rows, 128))

    def weigh(e, c, head, s_ref, m_ref):
        slot = (e * count + c) * 2 + head
        p = jnp.exp2(s_ref[slot] - m_ref[slot, :, :1]).astype(BF)
        o = jnp.dot(p, values[e], preferred_element_type=F32)
        return o[:, :128] / o[:, 128:]

    def phase(group, later, now, after):
        for e in range(width):
            load(width * group + e + pairs, values, e)
            if later is not None:
                load(width * later + e, keys, e)
        for e in range(width):
            for c in range(count):
                out = []
                for head in range(2):
                    if later is not None:
                        score(later, e, c, head, *after)
                    out.append(weigh(e, c, head, *now))
                o_refs[c][:, columns(width * group + e)] = jnp.where(low, out[0], out[1]).astype(BF)

    first, second = (s_a, m_a), (s_b, m_b)
    for e in range(width):
        load(e, keys, e)
        for c in range(count):
            for head in range(2):
                score(0, e, c, head, *first)

    def step(i, carry):
        phase(2 * i, 2 * i + 1, first, second)
        phase(2 * i + 1, 2 * i + 2, second, first)
        return carry

    lax.fori_loop(0, groups // 2 - 1, step, 0)
    phase(groups - 2, groups - 1, first, second)
    phase(groups - 1, None, second, first)


def spatial_attention(q, kvs, which):
    rows, total, count = q.shape[1], sum(kv.shape[0] for kv in kvs), len(which)
    width = 4
    heads = 2 * width * count
    whole = pl.BlockSpec(memory_space=pltpu.VMEM)
    return pl.pallas_call(
        functools.partial(spatial_kernel, which),
        in_specs=[whole] * (1 + len(kvs)),
        out_specs=[whole] * count,
        out_shape=[jax.ShapeDtypeStruct((rows, HW), BF)] * count,
        scratch_shapes=[pltpu.VMEM((width, total, 128), BF), pltpu.VMEM((width, total, 256), BF)]
        + [pltpu.VMEM((heads, rows, total), F32)] * 2
        + [pltpu.VMEM((heads, rows, 128), F32)] * 2,
        compiler_params=params(36),
        cost_estimate=pl.CostEstimate(
            flops=count * rows * total * HW,
            bytes_accessed=1_000_000,
            transcendentals=0,
        ),
        name="spatial_attention",
    )(q, *kvs)


def reorder(to_patch_major):
    row = lax.broadcasted_iota(jnp.int32, (64, 64), 0)
    col = lax.broadcasted_iota(jnp.int32, (64, 64), 1)
    if to_patch_major:
        return (col == (row % 4) * 16 + row // 4).astype(BF)
    return (col == (row % 16) * 4 + row // 16).astype(BF)


def home(scalars, d):
    return lax.rem(scalars[2] + 4 - d, 4)


def middle_of(scalars, f, s_ref, x_ref, w_ref):
    valid = (scalars[0] + f < scalars[1]).astype(F32)
    branch = jnp.dot(s_ref[...], w_ref[...], preferred_element_type=F32)
    return (x_ref[f].astype(F32) + valid * branch).astype(BF)


def early_kernel(distances, scalars, *refs):
    s_refs, (x_ref, w_ref, middle_ref, norm_ref) = refs[:-4], refs[-4:]
    for d, s_ref in zip(distances, s_refs):
        f = home(scalars, d)
        middle = middle_of(scalars, f, s_ref, x_ref, w_ref)
        middle_ref[f] = middle
        norm_ref[f] = normalise(middle.astype(F32))


def early_rows(scalars, blocks, distances, video, w):
    whole = pl.BlockSpec(memory_space=pltpu.VMEM)
    return pl.pallas_call(
        functools.partial(early_kernel, distances),
        in_specs=[pl.BlockSpec(memory_space=pltpu.SMEM)] + [whole] * (2 + len(blocks)),
        out_specs=[whole, whole],
        out_shape=[jax.ShapeDtypeStruct((4, 144, WIDTH), BF)] * 2,
        compiler_params=params(16),
        cost_estimate=pl.CostEstimate(
            flops=2 * len(blocks) * 144 * HW * WIDTH, bytes_accessed=8_000_000, transcendentals=0
        ),
        name="early_rows",
    )(scalars, *blocks, video, w)


def late_kernel(distance, scalars, s_ref, norm_ref, x_ref, w_ref, middle_ref, send_ref, late):
    last = home(scalars, distance)
    middle = middle_of(scalars, last, s_ref, x_ref, w_ref)
    middle_ref[...] = middle
    late[...] = normalise(middle.astype(F32))
    move = reorder(True)
    for b in range(9):
        rows = slice(b * 16, b * 16 + 16)
        parts = [jnp.where(last == f, late[rows, :], norm_ref[f, rows, :]) for f in range(4)]
        moved = jnp.dot(move, jnp.concatenate(parts, axis=0), preferred_element_type=F32)
        send_ref[rows] = moved.astype(BF).reshape(16, 4, WIDTH)


def late_rows(scalars, spatial, norm, distance, video, w):
    whole = pl.BlockSpec(memory_space=pltpu.VMEM)
    return pl.pallas_call(
        functools.partial(late_kernel, distance),
        in_specs=[pl.BlockSpec(memory_space=pltpu.SMEM)] + [whole] * 4,
        out_specs=[whole, whole],
        out_shape=[
            jax.ShapeDtypeStruct((144, WIDTH), BF),
            jax.ShapeDtypeStruct((144, 4, WIDTH), BF),
        ],
        scratch_shapes=[pltpu.VMEM((144, WIDTH), BF)],
        compiler_params=params(16),
        cost_estimate=pl.CostEstimate(
            flops=2 * 144 * HW * WIDTH, bytes_accessed=8_000_000, transcendentals=0
        ),
        name="late_rows",
    )(scalars, spatial, norm, video, w)


def temporal_kernel(n, scalars, x_ref, w_ref, o_ref, rows_ref):
    for i in range(n):
        rows_ref[64 * i : 64 * i + 64, :] = x_ref[:, i].reshape(64, WIDTH)
    limit = scalars[1]
    head_row = lax.broadcasted_iota(jnp.int32, (256, 256), 0) // HD
    head_col = lax.broadcasted_iota(jnp.int32, (256, 256), 1) // HD
    same = head_row == head_col
    zero = jnp.zeros((256, 256), BF)
    key_valid = lax.broadcasted_iota(jnp.int32, (4, 64, 64), 1) < limit

    def step(g, carry):
        def project(part):
            cols = pl.ds(pl.multiple_of(part * HW + g * 256, 128), 256)
            return jnp.dot(rows_ref[...], w_ref[:, cols], preferred_element_type=F32)

        q = (project(0) * QSCALE).astype(BF)
        k = project(1).astype(BF)
        v = project(2).astype(BF)
        scores, weights = [], []
        for i in range(n):
            rows = slice(64 * i, 64 * i + 64)
            k4 = jnp.where(same, jnp.concatenate([k[rows]] * 4, axis=0), zero)
            scores.append(nt_dot(k4, q[rows]).reshape(4, 64, 64))
        for i in range(n):
            s = jnp.where(key_valid, scores[i], -1e30)
            p = jnp.exp2(s - jnp.max(s, axis=1, keepdims=True))
            p = p / jnp.sum(p, axis=1, keepdims=True)
            weights.append(p.reshape(256, 64).astype(BF))
        cols = pl.ds(pl.multiple_of(g * 256, 128), 256)
        for i in range(n):
            rows = slice(64 * i, 64 * i + 64)
            v4 = jnp.where(same, jnp.concatenate([v[rows]] * 4, axis=0), zero)
            o_ref[:, i, :, cols] = tn_dot(weights[i], v4).astype(BF).reshape(16, 4, 256)
        return carry

    lax.fori_loop(0, 4, step, 0, unroll=4)


def temporal_attention(scalars, x, w, n):
    rows = 64 * n
    whole = pl.BlockSpec(memory_space=pltpu.VMEM)
    return pl.pallas_call(
        functools.partial(temporal_kernel, n),
        in_specs=[pl.BlockSpec(memory_space=pltpu.SMEM), whole, whole],
        out_specs=whole,
        out_shape=jax.ShapeDtypeStruct((TM, n, 4, HW), BF),
        scratch_shapes=[pltpu.VMEM((rows, WIDTH), BF)],
        compiler_params=params(24),
        cost_estimate=pl.CostEstimate(
            flops=2 * rows * WIDTH * 3 * HW, bytes_accessed=14_000_000, transcendentals=0
        ),
        name="temporal_attention",
    )(scalars, x, w)


def encoded_kernel(distance, scalars, t_ref, m_ref, late_ref, w_ref, o_ref, rows_ref, held, sem):
    last = home(scalars, distance)
    move = reorder(False)
    for b in range(9):
        block = t_ref[b * 16 : b * 16 + 16].reshape(64, HW)
        moved = jnp.dot(move, block, preferred_element_type=F32).astype(BF)
        for f in range(4):
            lo = f * 144 + b * 16
            rows_ref[lo : lo + 16, :] = moved[f * 16 : f * 16 + 16]
    first, limit = scalars[0], scalars[1]

    def leave(j):
        cols = pl.ds(pl.multiple_of(j * 256, 128), 256)
        return pltpu.make_async_copy(held.at[:, :, cols], o_ref.at[:, :, cols], sem.at[j])

    def project(j, carry):
        cols = pl.ds(pl.multiple_of(j * 256, 128), 256)
        branch = jnp.dot(rows_ref[...], w_ref[:, cols], preferred_element_type=F32)
        for f in range(4):
            valid = (first + f < limit).astype(F32)
            own = branch[f * 144 : (f + 1) * 144]
            middle = jnp.where(last == f, late_ref[:, cols], m_ref[f, :, cols])
            held[f, :, cols] = (middle.astype(F32) + valid * own).astype(BF)
        leave(j).start()
        return carry

    lax.fori_loop(0, 6, project, 0, unroll=3)
    for j in range(6):
        leave(j).wait()


def encoded_rows(scalars, temporal, middle, late, distance, w):
    whole = pl.BlockSpec(memory_space=pltpu.VMEM)
    return pl.pallas_call(
        functools.partial(encoded_kernel, distance),
        in_specs=[pl.BlockSpec(memory_space=pltpu.SMEM)] + [whole] * 4,
        out_specs=pl.BlockSpec(memory_space=pltpu.HBM),
        out_shape=jax.ShapeDtypeStruct((4, 144, WIDTH), BF),
        scratch_shapes=[
            pltpu.VMEM((4 * 144, HW), BF),
            pltpu.VMEM((4, 144, WIDTH), BF),
            pltpu.SemaphoreType.DMA((6,)),
        ],
        compiler_params=params(24),
        cost_estimate=pl.CostEstimate(
            flops=8 * 144 * HW * WIDTH, bytes_accessed=8_000_000, transcendentals=0
        ),
        name="encoded_rows",
    )(scalars, temporal, middle, late, w)


def along_z(x, distance):
    pairs = [(i, (i + 2 * distance) % 8) for i in range(8)]
    return lax.ppermute(x, "space", pairs)


def over_tm(x):
    return lax.all_to_all(x, "tm", split_axis=0, concat_axis=0, tiled=True)


def per_device(video, frame_count, qkv_space, out_space, qkv_time, out_time):
    first = lax.axis_index("tm") * video.shape[0]
    z = lax.axis_index("space") // 2
    scalars = jnp.stack([first, frame_count[0], z]).astype(jnp.int32)

    def from_chip(e, sent):
        return along_z(sent, 4 - e)

    sent = {
        e: lax.dynamic_index_in_dim(video, lax.rem(z + 4 - e, 4), 0, keepdims=False) for e in (1, 3, 2)
    }
    near = [from_chip(e, sent[e]) for e in (1, 3)]
    kv_own, q_own = own_block(scalars, video, qkv_space)
    kv_own_other = lax.ppermute(kv_own, "space", SWAP)
    late, kv_own, *near = lax.optimization_barrier((sent[2], kv_own, *near))
    far = from_chip(2, late)
    kv_near, q_near, w_held = near_blocks(near, qkv_space)
    kv_near_other = lax.ppermute(kv_near, "space", SWAP)
    far, kv_near = lax.optimization_barrier((far, kv_near))
    kv_far, norm1 = keys_values(far, w_held)
    kv_far_other = lax.ppermute(kv_far, "space", SWAP)
    q_far = queries(norm1, w_held)
    kvs = (kv_near, kv_far, kv_own, kv_near_other, kv_far_other, kv_own_other)
    back = {}
    for blocks in ((1, 3), (2,)):
        results = spatial_attention(q_near if 1 in blocks else q_far, kvs, range(len(blocks)))
        q_far, q_own, *results = lax.optimization_barrier((q_far, q_own, *results))
        for e, o in zip(blocks, results):
            back[e] = along_z(o, e)
    (back[0],) = spatial_attention(q_own, kvs, range(1))
    early = tuple(d for d in (0, 1, 2, 3) if d != LATE)
    middle, norm2 = early_rows(scalars, [back[d] for d in early], early, video, out_space)
    late, send = late_rows(scalars, back[LATE], norm2, LATE, video, out_space)
    rows = over_tm(send.reshape(TM, 9, 4, WIDTH))
    temporal = temporal_attention(scalars, rows, qkv_time, 9)
    temporal = over_tm(temporal).reshape(144, 4, HW)
    return encoded_rows(scalars, temporal, middle, late, LATE, out_time)


def solution(mesh):
    return jax.shard_map(
        per_device,
        mesh=mesh,
        in_specs=(P("tm", "space", None), P(), P(), P(), P(), P()),
        out_specs=P("tm", "space", None),
        check_vma=False,
    )
```
